32 devices in a mesh: parts: 2 (over x), rows: 16 (over z, y, core).
Axes of the slice: x: 2, y: 2, z: 4, core: 2. Of those that a mesh axis runs over, the one named last changes fastest.
Arguments:
- rhs: float32 [3, 12288, 256], P(None, 'rows', 'parts'), parts along dimension 2, may hold values from -6 to 6
- diag_inv: float32 [3, 12288, 768], P(None, 'rows'), may hold values from -0.21875 to 0.21875
- tiles: float32 [2, 32, 768, 768], P(None, 'rows'), may hold values from -0.15625 to 0.15625
- dest: int32 [2, 16, 2], P(None, 'rows'), may hold values from 0 to 15, all different within a row; in each aligned block of 16 rows (0 to 15, 16 to 31, ..., all dimensions but the last counted through in order) at most 4 rows name the same one
- obs_weight: float32 [12288], P('rows'), may hold values from -0.108253175 to 0.108253175, as said below
Outputs:
- solution: float32 [3, 12288, 256], P(None, 'rows', 'parts'), parts along dimension 2
- observed: float32 [256], P('parts'), parts along dimension 0
The draws below stay inside these ranges and needn't reach their ends.
There are 2 independent parts, one for each index of `parts`. The reference program is written for one: setup_inputs(seed, part) draws one part's arguments, and reference() takes and returns one part's arrays. A program takes and returns all parts, laid end to end along the dimension named above; an argument that names none is the same for every part. Nothing has to cross between parts.
Inputs may be any that keep to these rules, and one draw needn't show every extreme that they name: `dest`: in each of the two levels, the two entries of a supernode differ, and no supernode of the next level is named more than 4 times. `obs_weight`: finite weights.
All inputs are finite; a program needn't handle non-finite values.
Results may differ from the reference program's by a relative error of at most 0.00029.
Values sent between devices are 32-bit elements; how exact they have to be, the bound alone decides.
A program may use at most 128 MiB of HBM per device.

```python
import math
import jax
import jax.numpy as jnp
import numpy as np
from jax import lax

SN = 768
R = 128
CAP = 4
NSN = 16


def draw_obs_weight(key, part):
    total = NSN * SN
    position = jnp.arange(total, dtype=jnp.float32) / jnp.float32(max(total - 1, 1))
    base = jax.random.truncated_normal(key, -4.0, 4.0, (total,), jnp.float32)
    ramp = 1.0 + 2.0 * position
    return base * ramp / (3.0 * jnp.sqrt(jnp.float32(total)))


def block_levels(own_key, extent, pieces, smallest, high):
    loudness, own = 1.0, jax.random.fold_in(own_key, 6)
    for dim, shards_of in pieces:
        draws = jnp.exp(jax.random.uniform(jax.random.fold_in(own, dim), (shards_of,), jnp.float32, smallest / len(pieces), high / len(pieces)))
        loudness = loudness * jnp.repeat(draws, extent[dim] // shards_of).reshape([-1 if axis == dim else 1 for axis in range(len(extent))])
    return loudness


def deal_out(key, own, number, rows, number_of, top, limit, lean):
    sequence = jax.random.permutation(key, number_of)
    heavy_load, usual = shares(number_of, rows * top, limit, lean, True), shares(number_of, rows * top, limit, lean, False)
    places = jnp.arange(number_of)

    def named(lengths, turn):
        used = int((lengths > 0).sum())
        fixed = max(1, used // 4)
        passed = fixed + (places - fixed + turn * (used - fixed)) % max(1, number_of - fixed)
        return jnp.zeros((number_of,), jnp.int32).at[sequence[jnp.where(places < fixed, places, passed)]].set(jnp.asarray(lengths, jnp.int32))

    lengths = jnp.where(number % 4 == 0, named(heavy_load, number // 4), named(usual, number - number // 4 - 1))
    mixed = jax.random.permutation(jax.random.fold_in(own, 3), number_of)
    source_of, sink = mixed[0:number_of // 2 * 2:2], mixed[1:number_of // 2 * 2:2]
    slack = jnp.minimum(lengths[source_of] - 1, limit - lengths[sink]) // 2
    slack = jnp.where((source_of == sequence[0]) | (sink == sequence[0]) | (lengths[sink] == 0), 0, jnp.maximum(slack, 0))
    passed = jax.random.randint(jax.random.fold_in(own, 4), (number_of // 2,), 0, 1 << 20) % (slack + 1)
    lengths = lengths.at[source_of].add(-passed).at[sink].add(passed)
    members = jnp.searchsorted(jnp.cumsum(lengths), jnp.arange(rows * top), side="right").astype(jnp.int32)
    grid = members.reshape(top, rows).T
    grid = grid[jax.random.permutation(jax.random.fold_in(own, 1), rows)]
    turn = jax.random.randint(jax.random.fold_in(own, 2), (rows, 1), 0, top)
    return jnp.take_along_axis(grid, (jnp.arange(top)[None, :] + turn) % top, axis=1)


def shares(count, total, reach, lean, full):
    portions = [(1 << 20) // math.isqrt(rank ** lean) + 1 for rank in range(1, count + 1)]
    largest = reach if full else min(reach, max(-(-total // count), total * portions[0] // sum(portions)))
    least = 1 if total - largest >= count - 1 else 0
    holding, spare = [largest] + [least] * (count - 1), total - largest - least * (count - 1)
    while spare > 0:
        candidates = [i for i in range(1, count) if holding[i] < largest] or [i for i in range(1, count) if holding[i] < reach]
        whole, left = sum([portions[i] for i in candidates]), spare
        for i in candidates:
            extra = min(reach - holding[i], max(1, left * portions[i] // whole), spare)
            holding[i] = holding[i] + extra
            spare = spare - extra
    return np.array(holding)


def bell_draw(key, extent, scale, reach, pieces=(), held_as=jnp.bfloat16):
    drawn = jax.random.normal(key, extent, jnp.float32) * scale
    if len(pieces) > 0:
        drawn = block_levels(key, extent, pieces, -0.22, 0.18) * drawn
    return jnp.clip(drawn, min=-reach, max=reach).astype(held_as)


def setup_inputs(seed: int = 0, part: int = 0) -> dict:
    seeds = jax.random.split(jax.random.key(seed), 6)
    own_keys = jax.random.split(jax.random.fold_in(seeds[5], part), 6)
    rhs = bell_draw(own_keys[0], (3, NSN * SN, R), 1.0, 6.0, ((1, 16),), jnp.float32)
    diag_inv = bell_draw(seeds[1], (3, NSN * SN, SN), SN ** -0.5, 0.21875, ((1, 16),), jnp.float32)
    tiles = bell_draw(seeds[2], (2, NSN * 2, SN, SN), (2 * SN) ** -0.5, 0.15625, ((1, 16),), jnp.float32)
    dest_keys = jax.random.split(jax.random.fold_in(seeds[3], 1), 2 * NSN // NSN)
    dest_turns = jax.random.permutation(jax.random.fold_in(seeds[3], 3), 2 * NSN // NSN)
    dest = jax.vmap(lambda own, number: deal_out(jax.random.fold_in(seeds[3], 2), own, number, NSN, NSN, 2, CAP, 2))(dest_keys, dest_turns).reshape((2, NSN, 2))
    obs_weight = draw_obs_weight(jax.random.fold_in(seeds[5], 71), part)
    return {"rhs": rhs, "diag_inv": diag_inv, "tiles": tiles, "dest": dest, "obs_weight": obs_weight}


def solve_blocks(matrices, rights):
    def one_block(pair):
        return jnp.dot(pair[0], pair[1], precision=lax.Precision.HIGHEST, preferred_element_type=jnp.float32)
    return lax.map(one_block, (matrices, rights))


def reference(rhs, diag_inv, tiles, dest, obs_weight):
    blocks_rhs = rhs.reshape(3, NSN, SN, R)
    inverses = diag_inv.reshape(3, NSN, SN, SN)
    couplings = tiles.reshape(2, NSN, 2, SN, SN)
    solved = solve_blocks(inverses[0], blocks_rhs[0])
    levels = [solved]
    supernodes = jnp.arange(NSN, dtype=jnp.int32)
    for section in range(2):
        def tile_products(pair):
            return jnp.einsum('kab,bc->kac', pair[0], pair[1], precision=lax.Precision.HIGHEST, preferred_element_type=jnp.float32)
        products = lax.map(tile_products, (couplings[section], solved))
        matches = (dest[section][:, :, None] == supernodes[None, None, :]).astype(jnp.float32)
        update = jnp.einsum('jkd,jkac->dac', matches, products, precision=lax.Precision.HIGHEST)
        current = blocks_rhs[section + 1] - update
        solved = solve_blocks(inverses[section + 1], current)
        levels.append(solved)
    solution = jnp.stack(levels).reshape(3, NSN * SN, R)
    observed = jnp.dot(obs_weight, solution[2], precision=lax.Precision.HIGHEST, preferred_element_type=jnp.float32)
    return solution, observed
```

```python
import functools
import jax
import jax.numpy as jnp
from jax import lax
from jax.experimental import pallas as pl
from jax.experimental.pallas import tpu as pltpu
from jax.sharding import PartitionSpec as P

CAP = 4
PIECES = 4


def split(value):
    high = value.astype(jnp.bfloat16)
    return high, (value - high.astype(jnp.float32)).astype(jnp.bfloat16)


def dot_pair(high, low, right, width):
    wide = jnp.dot(high, right, preferred_element_type=jnp.float32)
    return (
        wide[:, :width]
        + wide[:, width:]
        + jnp.dot(low, right[:, :width], preferred_element_type=jnp.float32)
    )


def kernel(n, rhs, weight, dest, diag, tiles, sol, observed, *scratch):
    stage1 = [scratch[t * PIECES : (t + 1) * PIECES] for t in range(2)]
    (
        diag_f, tile_f, diag_hi, diag_lo, tile_hi, tile_lo, solved,
        send1, send2, recv2, own, send3, update, names, names_s, table, share, shares,
        load_sem, s1_send, s1_recv, s2_send, s2_recv, s3_send, s3_recv,
        n_send, n_recv, n_copy, o_send, o_recv,
    ) = scratch[2 * PIECES :]
    size, width = rhs.shape[1], rhs.shape[2]
    half, hubs = n // 2, n // 4
    block = size // PIECES
    rows = block // hubs
    me = lax.axis_index("rows")
    side = me // half
    base = side * half
    pos = me - base
    first_hub = (1 - side) * hubs
    is_hub = jnp.logical_and(pos >= first_hub, pos < first_hub + hubs)
    hub = pos - first_hub
    opposite = (1 - side) * half
    peer = me + hubs * (1 - 2 * side)

    barrier = pltpu.get_barrier_semaphore()
    for other in range(n):
        @pl.when(other != me)
        def _():
            pl.semaphore_signal(barrier, inc=1, device_id={"rows": other})

    loads = [pltpu.make_async_copy(diag.at[0], diag_f.at[0], load_sem.at[0])]
    loads += [pltpu.make_async_copy(tiles.at[0, k], tile_f.at[0, k], load_sem.at[1 + k]) for k in range(2)]
    loads += [pltpu.make_async_copy(diag.at[1], diag_f.at[1], load_sem.at[3])]
    loads += [pltpu.make_async_copy(tiles.at[1, k], tile_f.at[1, k], load_sem.at[4 + k]) for k in range(2)]
    loads += [pltpu.make_async_copy(diag.at[2], diag_f.at[2], load_sem.at[6])]
    for copy in loads:
        copy.start()

    strip = size // 8

    def split_into(source, high_ref, low_ref):
        def step(i, carry):
            at = pl.ds(pl.multiple_of(i * strip, strip), strip)
            high, low = split(source[at, :])
            high_ref[at, :] = high
            low_ref[at, :] = low
            return carry
        lax.fori_loop(0, 8, step, 0)

    def ready_diag(level):
        loads[3 * level].wait()
        split_into(diag_f.at[level], diag_hi.at[level], diag_lo.at[level])

    def ready_tiles(t):
        for k in range(2):
            loads[3 * t + 1 + k].wait()
            split_into(tile_f.at[t, k], tile_hi.at[t, k], tile_lo.at[t, k])

    def solve(level, current):
        high, low = split(current)
        right = jnp.concatenate([high, low], axis=1)
        solved[...] = right

        def step(i, carry):
            at = pl.ds(pl.multiple_of(i * block, block), block)
            sol[level, at, :] = dot_pair(diag_hi[level, at, :], diag_lo[level, at, :], solved[...], width)
            return carry
        lax.fori_loop(0, PIECES, step, 0)
        high, low = split(sol[level])
        solved[:, :width] = high
        solved[:, width:] = low

    def names_copy(p, slot):
        return pltpu.make_async_remote_copy(
            src_ref=share, dst_ref=names.at[slot], send_sem=n_send.at[p], recv_sem=n_recv.at[slot],
            device_id={"rows": base + first_hub + p})

    def first(t, c, p, slot):
        return pltpu.make_async_remote_copy(
            src_ref=send1.at[t, c, :, pl.ds(p * rows, rows), :],
            dst_ref=stage1[t][c].at[pl.ds(2 * slot, 2)],
            send_sem=s1_send.at[t, c, p], recv_sem=s1_recv.at[t, c, slot],
            device_id={"rows": base + first_hub + p})

    def second(t, c):
        return pltpu.make_async_remote_copy(
            src_ref=send2.at[t, c], dst_ref=recv2.at[t, c],
            send_sem=s2_send.at[t, c], recv_sem=s2_recv.at[t, c], device_id={"rows": peer})

    def third(t, c, owner, slot):
        at = pl.ds(c * block + slot * rows, rows)
        return pltpu.make_async_remote_copy(
            src_ref=send3.at[t, c, owner], dst_ref=update.at[t, at, :],
            send_sem=s3_send.at[t, c, owner], recv_sem=s3_recv.at[t, c, slot],
            device_id={"rows": base + owner})

    line = lax.broadcasted_iota(jnp.int32, share.shape, 0)
    lane = lax.broadcasted_iota(jnp.int32, share.shape, 1)
    value = jnp.zeros(share.shape, jnp.int32)
    for t in range(2):
        for k in range(2):
            value = jnp.where(jnp.logical_and(line == t, lane == k), dest[t, k], value)
    share[...] = value

    ready_diag(0)
    solve(0, rhs[0])
    ready_tiles(0)
    pl.semaphore_wait(barrier, n - 1)

    for p in range(hubs):
        mine = jnp.logical_and(is_hub, hub == p)

        @pl.when(jnp.logical_not(mine))
        def _():
            names_copy(p, pos).start()

        @pl.when(mine)
        def _():
            names[pos] = share[...]

    def build_table():
        for slot in range(half):
            @pl.when(slot != pos)
            def _():
                names_copy(0, slot).wait_recv()
        move = pltpu.make_async_copy(names, names_s, n_copy)
        move.start()
        move.wait()
        for t in range(2):
            def one(d, carry):
                count = jnp.int32(0)
                places = [jnp.int32(n)] * CAP
                for q in range(n):
                    hit = names_s[q // 2, t, q % 2] == d
                    for r in range(CAP):
                        places[r] = jnp.where(jnp.logical_and(hit, count == r), q, places[r])
                    count = count + jnp.where(hit, 1, 0)
                for r in range(CAP):
                    table[t, d * CAP + r] = places[r]
                return carry
            lax.fori_loop(0, n, one, 0)

    def add_up(t, c, start, out):
        buffer = stage1[t][c]

        def one(i, carry):
            at = (start + i) * CAP
            total = buffer[table[t, at]] + buffer[table[t, at + 1]]
            out[i] = total + (buffer[table[t, at + 2]] + buffer[table[t, at + 3]])
            return carry
        lax.fori_loop(0, half, one, 0)

    for t in range(2):
        for c in range(PIECES):
            for k in range(2):
                at = pl.ds(c * block, block)
                send1[t, c, k] = dot_pair(tile_hi[t, k, at, :], tile_lo[t, k, at, :], solved[...], width)
            for p in range(hubs):
                mine = jnp.logical_and(is_hub, hub == p)

                @pl.when(jnp.logical_not(mine))
                def _():
                    first(t, c, p, pos).start()

                @pl.when(mine)
                def _():
                    stage1[t][c][pl.ds(2 * pos, 2)] = send1[t, c, :, p * rows : (p + 1) * rows, :]
        ready_diag(t + 1)
        if t == 0:
            ready_tiles(1)

        @pl.when(is_hub)
        def _():
            if t == 0:
                build_table()

            def finish(c):
                second(t, c).wait_recv()

                def one(i, carry):
                    send3[t, c, i] = own[c % 2, i] + recv2[t, c, i]
                    return carry
                lax.fori_loop(0, half, one, 0)
                for owner in range(half):
                    @pl.when(owner != pos)
                    def _():
                        third(t, c, owner, hub).start()
                update[t, pl.ds(c * block + hub * rows, rows), :] = send3[t, c, pos]

            for c in range(PIECES):
                stage1[t][c][n] = jnp.zeros((rows, width), jnp.float32)
                for slot in range(half):
                    @pl.when(slot != pos)
                    def _():
                        first(t, c, 0, slot).wait_recv()
                add_up(t, c, opposite, send2.at[t, c])
                second(t, c).start()
                add_up(t, c, base, own.at[c % 2])
                if c > 0:
                    finish(c - 1)
            finish(PIECES - 1)

        for c in range(PIECES):
            for p in range(hubs):
                @pl.when(jnp.logical_not(jnp.logical_and(is_hub, hub == p)))
                def _():
                    third(t, c, 0, p).wait_recv()
        solve(t + 1, rhs[t + 1] - update[t])

    high, low = split(jnp.broadcast_to(weight[...], (16, size)))
    part = dot_pair(high, low, solved[...], width)
    shares[me] = part[:8]

    def total_copy(other, slot):
        return pltpu.make_async_remote_copy(
            src_ref=shares.at[me], dst_ref=shares.at[me], send_sem=o_send.at[other], recv_sem=o_recv.at[slot],
            device_id={"rows": other})

    for other in range(n):
        @pl.when(other != me)
        def _():
            total_copy(other, me).start()

    for p in range(hubs):
        @pl.when(jnp.logical_not(jnp.logical_and(is_hub, hub == p)))
        def _():
            names_copy(p, pos).wait_send()
            for t in range(2):
                for c in range(PIECES):
                    first(t, c, p, pos).wait_send()

    @pl.when(is_hub)
    def _():
        for t in range(2):
            for c in range(PIECES):
                second(t, c).wait_send()
                for owner in range(half):
                    @pl.when(owner != pos)
                    def _():
                        third(t, c, owner, hub).wait_send()

    for other in range(n):
        @pl.when(other != me)
        def _():
            pltpu.make_async_remote_copy(
                src_ref=shares.at[other], dst_ref=shares.at[other], send_sem=o_send.at[other],
                recv_sem=o_recv.at[other], device_id={"rows": other}).wait()
    total = shares[0]
    for other in range(1, n):
        total = total + shares[other]
    observed[...] = total[:1]


def body(rhs, diag_inv, tiles, dest, obs_weight):
    n = lax.axis_size("rows")
    size, width = rhs.shape[1], rhs.shape[2]
    half, hubs = n // 2, n // 4
    rows = size // PIECES // hubs
    f32, bf16 = jnp.float32, jnp.bfloat16
    dma = pltpu.SemaphoreType.DMA
    vmem = pl.BlockSpec(memory_space=pltpu.VMEM)
    anywhere = pl.BlockSpec(memory_space=pl.ANY)
    sol, observed = pl.pallas_call(
        functools.partial(kernel, n),
        out_shape=(
            jax.ShapeDtypeStruct((3, size, width), f32),
            jax.ShapeDtypeStruct((1, width), f32),
        ),
        in_specs=[vmem, vmem, pl.BlockSpec(memory_space=pltpu.SMEM), anywhere, anywhere],
        out_specs=(vmem, vmem),
        scratch_shapes=[pltpu.VMEM((n + 1, rows, width), f32) for _ in range(2 * PIECES)] + [
            pltpu.VMEM((3, size, size), f32),
            pltpu.VMEM((2, 2, size, size), f32),
            pltpu.VMEM((3, size, size), bf16),
            pltpu.VMEM((3, size, size), bf16),
            pltpu.VMEM((2, 2, size, size), bf16),
            pltpu.VMEM((2, 2, size, size), bf16),
            pltpu.VMEM((size, 2 * width), bf16),
            pltpu.VMEM((2, PIECES, 2, size // PIECES, width), f32),
            pltpu.VMEM((2, PIECES, half, rows, width), f32),
            pltpu.VMEM((2, PIECES, half, rows, width), f32),
            pltpu.VMEM((2, half, rows, width), f32),
            pltpu.VMEM((2, PIECES, half, rows, width), f32),
            pltpu.VMEM((2, size, width), f32),
            pltpu.VMEM((half, 8, 128), jnp.int32),
            pltpu.SMEM((half, 8, 128), jnp.int32),
            pltpu.SMEM((2, n * CAP), jnp.int32),
            pltpu.VMEM((8, 128), jnp.int32),
            pltpu.VMEM((n, 8, width), f32),
            dma((7,)),
            dma((2, PIECES, hubs)), dma((2, PIECES, half)),
            dma((2, PIECES)), dma((2, PIECES)),
            dma((2, PIECES, half)), dma((2, PIECES, hubs)),
            dma((hubs,)), dma((half,)), dma,
            dma((n,)), dma((n,)),
        ],
        compiler_params=pltpu.CompilerParams(
            collective_id=0, has_side_effects=True, vmem_limit_bytes=56 * 1024 * 1024
        ),
        cost_estimate=pl.CostEstimate(
            flops=7 * 3 * 2 * size * size * width, bytes_accessed=7 * 4 * size * size, transcendentals=0
        ),
    )(rhs, obs_weight.reshape(1, size), dest.reshape(2, 2), diag_inv, tiles)
    return sol, observed.reshape(width)


def solution(mesh):
    in_specs = (
        P(None, "rows", "parts"),
        P(None, "rows", None),
        P(None, "rows", None, None),
        P(None, "rows", None),
        P("rows"),
    )
    out_specs = (P(None, "rows", "parts"), P("parts"))
    return jax.shard_map(body, mesh=mesh, in_specs=in_specs, out_specs=out_specs, check_vma=False)
```

```python
import functools
import jax
import jax.numpy as jnp
from jax import lax
from jax.experimental import pallas as pl
from jax.experimental.pallas import tpu as pltpu
from jax.sharding import PartitionSpec as P

CAP = 4
PIECES = 3


def split(value):
    high = value.astype(jnp.bfloat16)
    return high, (value - high.astype(jnp.float32)).astype(jnp.bfloat16)


def kernel(n, pieces, rhs, weight, dest, diag, tiles, sol, observed, *scratch):
    stage1 = [scratch[p * pieces : (p + 1) * pieces] for p in range(4)]
    (
        rhs_v, diag_f, tile_f, diag_hi, diag_lo, tile_hi, tile_lo, solved, sol_v,
        send1, send2, recv2, own, send3, update, share, names, places_v, table, shares,
        load_sem, out_sem, s1_send, s1_recv, s2_send, s2_recv, s3_send, s3_recv,
        n_send, n_recv, n_copy, o_send, o_recv,
    ) = scratch[4 * pieces :]
    size, width = rhs.shape[1], rhs.shape[2]
    half, hubs = n // 2, n // 4
    block = size // pieces
    packed = block // 2
    rows = packed // hubs
    me = lax.axis_index("rows")
    side = me // half
    base = side * half
    pos = me - base
    first_hub = (1 - side) * hubs
    is_hub = jnp.logical_and(pos >= first_hub, pos < first_hub + hubs)
    hub = pos - first_hub
    opposite = (1 - side) * half
    peer = me + hubs * (1 - 2 * side)

    barrier = pltpu.get_barrier_semaphore()
    for other in range(n):
        @pl.when(other != me)
        def _():
            pl.semaphore_signal(barrier, inc=1, device_id={"rows": other})

    loads = []

    def load(source, target):
        loads.append(pltpu.make_async_copy(source, target, load_sem.at[len(loads)]))
        loads[-1].start()

    for level in range(3):
        load(rhs.at[level], rhs_v.at[level])
        load(diag.at[level], diag_f.at[level])
        if level < 2:
            for k in range(2):
                load(tiles.at[level, k], tile_f.at[level, k])

    strip = size // 8

    def split_into(source, high_ref, low_ref):
        def step(i, carry):
            at = pl.ds(pl.multiple_of(i * strip, strip), strip)
            high, low = split(source[at, :])
            high_ref[at, :] = high
            low_ref[at, :] = low
            return carry
        lax.fori_loop(0, 8, step, 0)

    def ready_diag(level):
        loads[4 * level].wait()
        loads[4 * level + 1].wait()
        split_into(diag_f.at[level], diag_hi.at[level], diag_lo.at[level])

    def ready_tiles(level):
        for k in range(2):
            loads[4 * level + 2 + k].wait()
            split_into(tile_f.at[level, k], tile_hi.at[level, k], tile_lo.at[level, k])

    def left(shape):
        return lax.broadcasted_iota(jnp.int32, shape, 1) < width // 2

    def swap(value):
        return pltpu.roll(value, width // 2, 1)

    def twice(value, h):
        low, high = (value, swap(value)) if h == 0 else (swap(value), value)
        return jnp.where(left(value.shape), low, high)

    def keep(h, value):
        high, low = split(value)
        mask = left(value.shape)
        both = jnp.where(mask, high.astype(jnp.float32), low.astype(jnp.float32))
        solved[h, :, :width] = both.astype(jnp.bfloat16)
        solved[h, :, width:] = high

    def multiply(high, low, h):
        wide = jnp.dot(high, solved[h, :, :width], preferred_element_type=jnp.float32)
        return wide + swap(wide) + jnp.dot(low, solved[h, :, width:], preferred_element_type=jnp.float32)

    def solve(level, h, current):
        keep(h, current)
        for c in range(pieces):
            at = pl.ds(c * block, block)
            sol_v[h, at, :] = multiply(diag_hi[level, at, :], diag_lo[level, at, :], h)
        value = sol_v[h]
        keep(h, value)
        if h == 0:
            mixed = jnp.where(left(value.shape), value, rhs_v[level])
        else:
            mixed = jnp.where(left(value.shape), rhs_v[level], value)
        rhs_v[level] = mixed

    def result_copy(level):
        return pltpu.make_async_copy(rhs_v.at[level], sol.at[level], out_sem.at[level])

    def names_copy(p, slot):
        return pltpu.make_async_remote_copy(
            src_ref=share, dst_ref=names.at[slot], send_sem=n_send.at[p], recv_sem=n_recv.at[slot],
            device_id={"rows": base + first_hub + p})

    def first(p, c, to, slot):
        return pltpu.make_async_remote_copy(
            src_ref=send1.at[p, c, :, pl.ds(to * rows, rows), :],
            dst_ref=stage1[p][c].at[pl.ds(2 * slot, 2)],
            send_sem=s1_send.at[p, c, to], recv_sem=s1_recv.at[p, c, slot],
            device_id={"rows": base + first_hub + to})

    def second(p, c):
        return pltpu.make_async_remote_copy(
            src_ref=send2.at[p, c], dst_ref=recv2.at[p, c],
            send_sem=s2_send.at[p, c], recv_sem=s2_recv.at[p, c], device_id={"rows": peer})

    def third(p, c, owner, slot):
        return pltpu.make_async_remote_copy(
            src_ref=send3.at[p, c, owner], dst_ref=update.at[p, c, pl.ds(slot * rows, rows), :],
            send_sem=s3_send.at[p, c, owner], recv_sem=s3_recv.at[p, c, slot],
            device_id={"rows": base + owner})

    def send_products(p):
        t, h = p // 2, p % 2
        for c in range(pieces):
            at = pl.ds(c * block, block)
            for k in range(2):
                value = multiply(tile_hi[t, k, at, :], tile_lo[t, k, at, :], h)
                top, bottom = value[:packed], value[packed:]
                send1[p, c, k] = jnp.where(left(top.shape), top, bottom)
            for to in range(hubs):
                mine = jnp.logical_and(is_hub, hub == to)

                @pl.when(jnp.logical_not(mine))
                def _():
                    first(p, c, to, pos).start()

                @pl.when(mine)
                def _():
                    stage1[p][c][pl.ds(2 * pos, 2)] = send1[p, c, :, to * rows : (to + 1) * rows, :]

    def build_table():
        for slot in range(half):
            @pl.when(slot != pos)
            def _():
                names_copy(0, slot).wait_recv()
        shape = places_v.shape
        target = lax.broadcasted_iota(jnp.int32, shape, 0)
        turn = lax.broadcasted_iota(jnp.int32, shape, 1) % CAP
        count = jnp.zeros(shape, jnp.int32)
        place = jnp.full(shape, n, jnp.int32)
        for q in range(n):
            hit = jnp.broadcast_to(names[q // 2, q % 2 : q % 2 + 1, :], shape) == target
            place = jnp.where(jnp.logical_and(hit, count == turn), q, place)
            count = count + jnp.where(hit, 1, 0)
        places_v[...] = place
        move = pltpu.make_async_copy(places_v, table, n_copy)
        move.start()
        move.wait()

    def add_up(p, c, start, out):
        buffer, column = stage1[p][c], p // 2 * CAP

        def one(i, carry):
            d = start + i
            total = buffer[table[d, column]] + buffer[table[d, column + 1]]
            out[i] = total + (buffer[table[d, column + 2]] + buffer[table[d, column + 3]])
            return carry
        lax.fori_loop(0, half, one, 0)

    def finish(step):
        p, c = step // pieces, step % pieces
        second(p, c).wait_recv()

        def one(i, carry):
            send3[p, c, i] = own[step % 2, i] + recv2[p, c, i]
            return carry
        lax.fori_loop(0, half, one, 0)
        for owner in range(half):
            @pl.when(owner != pos)
            def _():
                third(p, c, owner, hub).start()
        update[p, c, pl.ds(hub * rows, rows), :] = send3[p, c, pos]

    def hub_step(step):
        p, c = step // pieces, step % pieces

        @pl.when(is_hub)
        def _():
            if step == 0:
                build_table()
            if step < 4 * pieces:
                for slot in range(half):
                    @pl.when(slot != pos)
                    def _():
                        first(p, c, 0, slot).wait_recv()
                add_up(p, c, opposite, send2.at[p, c])
                second(p, c).start()
                add_up(p, c, base, own.at[step % 2])
            if step > 0:
                finish(step - 1)

    def receive(p):
        t, h = p // 2, p % 2
        for c in range(pieces):
            for slot in range(hubs):
                @pl.when(jnp.logical_not(jnp.logical_and(is_hub, hub == slot)))
                def _():
                    third(p, c, 0, slot).wait_recv()
        parts = []
        for c in range(pieces):
            value = update[p, c]
            parts += [twice(value, 0), twice(value, 1)]
        solve(t + 1, h, twice(rhs_v[t + 1], h) - jnp.concatenate(parts, axis=0))

    line = lax.broadcasted_iota(jnp.int32, share.shape, 0)
    lane = lax.broadcasted_iota(jnp.int32, share.shape, 1)
    value = jnp.zeros(share.shape, jnp.int32)
    for k in range(2):
        value = jnp.where(line == k, jnp.where(lane < CAP, dest[0, k], dest[1, k]), value)
    share[...] = value
    for p in range(4):
        for c in range(pieces):
            stage1[p][c][n] = jnp.zeros((rows, width), jnp.float32)

    ready_diag(0)
    solve(0, 0, twice(rhs_v[0], 0))
    pl.semaphore_wait(barrier, n - 1)
    for to in range(hubs):
        mine = jnp.logical_and(is_hub, hub == to)

        @pl.when(jnp.logical_not(mine))
        def _():
            names_copy(to, pos).start()

        @pl.when(mine)
        def _():
            names[pos] = share[...]
    ready_tiles(0)
    send_products(0)
    solve(0, 1, twice(rhs_v[0], 1))
    result_copy(0).start()
    send_products(1)

    for step in range(4 * pieces + 1):
        hub_step(step)
        if step == 0:
            ready_diag(1)
            ready_tiles(1)
        if step == 2 * pieces:
            ready_diag(2)
        if step == pieces + 1:
            receive(0)
            send_products(2)
        if step == 2 * pieces + 1:
            receive(1)
            result_copy(1).start()
            send_products(3)
        if step == 3 * pieces + 1:
            receive(2)
    receive(3)
    result_copy(2).start()

    high, low = split(jnp.broadcast_to(weight[...].reshape(1, size), (16, size)))
    part = [multiply(high, low, h)[:8] for h in range(2)]
    shares[me] = jnp.where(left(part[0].shape), part[0], part[1])

    for other in range(n):
        @pl.when(other != me)
        def _():
            pltpu.make_async_remote_copy(
                src_ref=shares.at[me], dst_ref=shares.at[me], send_sem=o_send.at[other],
                recv_sem=o_recv.at[me], device_id={"rows": other}).start()

    for to in range(hubs):
        @pl.when(jnp.logical_not(jnp.logical_and(is_hub, hub == to)))
        def _():
            names_copy(to, pos).wait_send()
            for p in range(4):
                for c in range(pieces):
                    first(p, c, to, pos).wait_send()

    @pl.when(is_hub)
    def _():
        for p in range(4):
            for c in range(pieces):
                second(p, c).wait_send()
                for owner in range(half):
                    @pl.when(owner != pos)
                    def _():
                        third(p, c, owner, hub).wait_send()

    for other in range(n):
        @pl.when(other != me)
        def _():
            pltpu.make_async_remote_copy(
                src_ref=shares.at[other], dst_ref=shares.at[other], send_sem=o_send.at[other],
                recv_sem=o_recv.at[other], device_id={"rows": other}).wait()
    total = shares[0]
    for other in range(1, n):
        total = total + shares[other]
    observed[...] = total[:1]
    for level in range(3):
        result_copy(level).wait()


def body(rhs, diag_inv, tiles, dest, obs_weight):
    n = lax.axis_size("rows")
    size, width = rhs.shape[1], rhs.shape[2]
    half, hubs = n // 2, n // 4
    pieces = PIECES
    packed = size // pieces // 2
    rows = packed // hubs
    f32, bf16 = jnp.float32, jnp.bfloat16
    dma = pltpu.SemaphoreType.DMA
    vmem = pl.BlockSpec(memory_space=pltpu.VMEM)
    anywhere = pl.BlockSpec(memory_space=pl.ANY)
    sol, observed = pl.pallas_call(
        functools.partial(kernel, n, pieces),
        out_shape=(
            jax.ShapeDtypeStruct((3, size, width), f32),
            jax.ShapeDtypeStruct((1, width), f32),
        ),
        in_specs=[anywhere, vmem, pl.BlockSpec(memory_space=pltpu.SMEM), anywhere, anywhere],
        out_specs=(anywhere, vmem),
        scratch_shapes=[pltpu.VMEM((n + 1, rows, width), f32) for _ in range(4 * pieces)] + [
            pltpu.VMEM((3, size, width), f32),
            pltpu.VMEM((3, size, size), f32),
            pltpu.VMEM((2, 2, size, size), f32),
            pltpu.VMEM((3, size, size), bf16),
            pltpu.VMEM((3, size, size), bf16),
            pltpu.VMEM((2, 2, size, size), bf16),
            pltpu.VMEM((2, 2, size, size), bf16),
            pltpu.VMEM((2, size, 2 * width), bf16),
            pltpu.VMEM((2, size, width), f32),
            pltpu.VMEM((4, pieces, 2, packed, width), f32),
            pltpu.VMEM((4, pieces, half, rows, width), f32),
            pltpu.VMEM((4, pieces, half, rows, width), f32),
            pltpu.VMEM((2, half, rows, width), f32),
            pltpu.VMEM((4, pieces, half, rows, width), f32),
            pltpu.VMEM((4, pieces, packed, width), f32),
            pltpu.VMEM((8, 128), jnp.int32),
            pltpu.VMEM((half, 8, 128), jnp.int32),
            pltpu.VMEM((n, 128), jnp.int32),
            pltpu.SMEM((n, 128), jnp.int32),
            pltpu.VMEM((n, 8, width), f32),
            dma((10,)), dma((3,)),
            dma((4, pieces, hubs)), dma((4, pieces, half)),
            dma((4, pieces)), dma((4, pieces)),
            dma((4, pieces, half)), dma((4, pieces, hubs)),
            dma((hubs,)), dma((half,)), dma,
            dma((n,)), dma((n,)),
        ],
        compiler_params=pltpu.CompilerParams(
            collective_id=0, has_side_effects=True, vmem_limit_bytes=60 * 1024 * 1024
        ),
        cost_estimate=pl.CostEstimate(
            flops=7 * 3 * 2 * size * size * width, bytes_accessed=7 * 4 * size * size, transcendentals=0
        ),
    )(rhs, obs_weight, dest.reshape(2, 2), diag_inv, tiles)
    return sol, observed.reshape(width)


def solution(mesh):
    in_specs = (
        P(None, "rows", "parts"),
        P(None, "rows", None),
        P(None, "rows", None, None),
        P(None, "rows", None),
        P("rows"),
    )
    out_specs = (P(None, "rows", "parts"), P("parts"))
    return jax.shard_map(body, mesh=mesh, in_specs=in_specs, out_specs=out_specs, check_vma=False)
```

```python
import functools
import jax
import jax.numpy as jnp
from jax import lax
from jax.experimental import pallas as pl
from jax.experimental.pallas import tpu as pltpu
from jax.sharding import PartitionSpec as P

CAP = 4
PIECES = 3


def split(value):
    high = value.astype(jnp.bfloat16)
    return high, (value - high.astype(jnp.float32)).astype(jnp.bfloat16)


def kernel(n, pieces, rhs, weight, dest, diag, tiles, sol, observed, *scratch):
    stage1 = [scratch[p * pieces : (p + 1) * pieces] for p in range(4)]
    (
        rhs_v, diag_f, tile_f, diag_hi, diag_lo, tile_hi, tile_lo, solved, sol_v,
        send1, send2, recv2, own, send3, update, share, names, places_v, table, shares,
        load_sem, out_sem, s1_send, s1_recv, s2_send, s2_recv, s3_send, s3_recv,
        n_send, n_recv, n_copy, o_send, o_recv,
    ) = scratch[4 * pieces :]
    size, width = rhs.shape[1], rhs.shape[2]
    half, hubs = n // 2, n // 4
    block = size // pieces
    packed = block // 2
    rows = packed // hubs
    me = lax.axis_index("rows")
    side = me // half
    base = side * half
    pos = me - base
    first_hub = (1 - side) * hubs
    is_hub = jnp.logical_and(pos >= first_hub, pos < first_hub + hubs)
    hub = pos - first_hub
    opposite = (1 - side) * half
    peer = me + hubs * (1 - 2 * side)

    barrier = pltpu.get_barrier_semaphore()
    for j in range(1, n):
        pl.semaphore_signal(barrier, inc=1, device_id={"rows": lax.rem(me + j, n)})

    def await_bytes(ref, sem):
        pltpu.make_async_copy(ref, ref, sem).wait()

    loads = []

    def load(source, target):
        loads.append(pltpu.make_async_copy(source, target, load_sem.at[len(loads)]))

    for level in range(3):
        load(rhs.at[level], rhs_v.at[level])
        load(diag.at[level], diag_f.at[level])
        if level < 2:
            for k in range(2):
                load(tiles.at[level, k], tile_f.at[level, k])
    for copy in loads[:4]:
        copy.start()

    strip = size // 8

    def split_into(source, high_ref, low_ref):
        def step(i, carry):
            at = pl.ds(pl.multiple_of(i * strip, strip), strip)
            high, low = split(source[at, :])
            high_ref[at, :] = high
            low_ref[at, :] = low
            return carry
        lax.fori_loop(0, 8, step, 0)

    def ready_diag(level):
        loads[4 * level].wait()
        loads[4 * level + 1].wait()
        split_into(diag_f.at[level], diag_hi.at[level], diag_lo.at[level])

    def ready_tiles(level):
        for k in range(2):
            loads[4 * level + 2 + k].wait()
            split_into(tile_f.at[level, k], tile_hi.at[level, k], tile_lo.at[level, k])

    def left(shape):
        return lax.broadcasted_iota(jnp.int32, shape, 1) < width // 2

    def swap(value):
        return pltpu.roll(value, width // 2, 1)

    def twice(value, h):
        low, high = (value, swap(value)) if h == 0 else (swap(value), value)
        return jnp.where(left(value.shape), low, high)

    def keep(h, value):
        high, low = split(value)
        mask = left(value.shape)
        both = jnp.where(mask, high.astype(jnp.float32), low.astype(jnp.float32))
        solved[h, :, :width] = both.astype(jnp.bfloat16)
        solved[h, :, width:] = high

    def multiply(high, low, h):
        wide = jnp.dot(high, solved[h, :, :width], preferred_element_type=jnp.float32)
        return wide + swap(wide) + jnp.dot(low, solved[h, :, width:], preferred_element_type=jnp.float32)

    def solve(level, h, current):
        keep(h, current)
        for c in range(pieces):
            at = pl.ds(c * block, block)
            sol_v[h, at, :] = multiply(diag_hi[level, at, :], diag_lo[level, at, :], h)
        value = sol_v[h]
        keep(h, value)
        if h == 0:
            mixed = jnp.where(left(value.shape), value, rhs_v[level])
        else:
            mixed = jnp.where(left(value.shape), rhs_v[level], value)
        rhs_v[level] = mixed

    def result_copy(level):
        return pltpu.make_async_copy(rhs_v.at[level], sol.at[level], out_sem.at[level])

    def names_copy(to):
        return pltpu.make_async_remote_copy(
            src_ref=share, dst_ref=names.at[pos], send_sem=n_send, recv_sem=n_recv,
            device_id={"rows": base + first_hub + to})

    def first(p, c, to):
        return pltpu.make_async_remote_copy(
            src_ref=send1.at[p, c, :, pl.ds(pl.multiple_of(to * rows, rows), rows), :],
            dst_ref=stage1[p][c].at[pl.ds(2 * pos, 2)],
            send_sem=s1_send.at[p], recv_sem=s1_recv.at[p, c],
            device_id={"rows": base + first_hub + to})

    def second(p, c):
        return pltpu.make_async_remote_copy(
            src_ref=send2.at[p, c], dst_ref=recv2.at[p, c],
            send_sem=s2_send.at[p, c], recv_sem=s2_recv.at[p, c], device_id={"rows": peer})

    def third(p, c, owner):
        at = pl.ds(pl.multiple_of(hub * rows, rows), rows)
        return pltpu.make_async_remote_copy(
            src_ref=send3.at[p, c, owner], dst_ref=update.at[p, c, at, :],
            send_sem=s3_send.at[p], recv_sem=s3_recv.at[p],
            device_id={"rows": base + owner})

    def send_products(p):
        t, h = p // 2, p % 2
        for c in range(pieces):
            at = pl.ds(c * block, block)
            for k in range(2):
                value = multiply(tile_hi[t, k, at, :], tile_lo[t, k, at, :], h)
                top, bottom = value[:packed], value[packed:]
                send1[p, c, k] = jnp.where(left(top.shape), top, bottom)
            @pl.when(is_hub)
            def _():
                at = pl.ds(pl.multiple_of(hub * rows, rows), rows)
                stage1[p][c][pl.ds(2 * pos, 2)] = send1[p, c, :, at, :]

            @pl.when(jnp.logical_not(is_hub))
            def _():
                first(p, c, lax.rem(pos, hubs)).start()

            for j in range(1, hubs):
                first(p, c, lax.rem(pos + j, hubs)).start()

    def build_table():
        await_bytes(names.at[pl.ds(0, half - 1)], n_recv)
        shape = places_v.shape
        target = lax.broadcasted_iota(jnp.int32, shape, 0)
        turn = lax.broadcasted_iota(jnp.int32, shape, 1) % CAP
        count = jnp.zeros(shape, jnp.int32)
        place = jnp.full(shape, n, jnp.int32)
        for q in range(n):
            hit = jnp.broadcast_to(names[q // 2, q % 2 : q % 2 + 1, :], shape) == target
            place = jnp.where(jnp.logical_and(hit, count == turn), q, place)
            count = count + jnp.where(hit, 1, 0)
        places_v[...] = place
        move = pltpu.make_async_copy(places_v, table, n_copy)
        move.start()
        move.wait()

    def add_up(p, c, start, out):
        buffer, column = stage1[p][c], p // 2 * CAP

        for i in range(half):
            d = start + i
            total = buffer[table[d, column]] + buffer[table[d, column + 1]]
            out[i] = total + (buffer[table[d, column + 2]] + buffer[table[d, column + 3]])

    def finish(step):
        p, c = step // pieces, step % pieces
        second(p, c).wait_recv()

        for i in range(half):
            send3[p, c, i] = own[step % 2, i] + recv2[p, c, i]
        for j in range(1, half):
            third(p, c, lax.rem(pos + j, half)).start()
        update[p, c, pl.ds(pl.multiple_of(hub * rows, rows), rows), :] = send3[p, c, pos]

    def hub_step(step):
        p, c = step // pieces, step % pieces

        @pl.when(is_hub)
        def _():
            if step == 0:
                build_table()
            if step < 4 * pieces:
                await_bytes(stage1[p][c].at[pl.ds(0, 2 * (half - 1))], s1_recv.at[p, c])
                add_up(p, c, opposite, send2.at[p, c])
                second(p, c).start()
                add_up(p, c, base, own.at[step % 2])
            if step > 0:
                finish(step - 1)

    def receive(p):
        t, h = p // 2, p % 2
        @pl.when(is_hub)
        def _():
            await_bytes(update.at[p, :, pl.ds(0, packed - rows), :], s3_recv.at[p])

        @pl.when(jnp.logical_not(is_hub))
        def _():
            await_bytes(update.at[p], s3_recv.at[p])

        parts = []
        for c in range(pieces):
            value = update[p, c]
            parts += [twice(value, 0), twice(value, 1)]
        solve(t + 1, h, twice(rhs_v[t + 1], h) - jnp.concatenate(parts, axis=0))

    line = lax.broadcasted_iota(jnp.int32, share.shape, 0)
    lane = lax.broadcasted_iota(jnp.int32, share.shape, 1)
    value = jnp.zeros(share.shape, jnp.int32)
    for k in range(2):
        value = jnp.where(line == k, jnp.where(lane < CAP, dest[0, k], dest[1, k]), value)
    share[...] = value
    for p in range(4):
        for c in range(pieces):
            stage1[p][c][n] = jnp.zeros((rows, width), jnp.float32)

    ready_diag(0)
    solve(0, 0, twice(rhs_v[0], 0))
    pl.semaphore_wait(barrier, n - 1)
    @pl.when(is_hub)
    def _():
        names[pos] = share[...]

    @pl.when(jnp.logical_not(is_hub))
    def _():
        names_copy(lax.rem(pos, hubs)).start()

    for j in range(1, hubs):
        names_copy(lax.rem(pos + j, hubs)).start()
    ready_tiles(0)
    for copy in loads[4:]:
        copy.start()
    send_products(0)
    solve(0, 1, twice(rhs_v[0], 1))
    result_copy(0).start()
    send_products(1)

    for step in range(4 * pieces + 1):
        hub_step(step)
        if step == 0:
            ready_diag(1)
            ready_tiles(1)
        if step == 2 * pieces:
            ready_diag(2)
        if step == pieces + 1:
            receive(0)
            send_products(2)
        if step == 2 * pieces + 1:
            receive(1)
            result_copy(1).start()
            send_products(3)
        if step == 3 * pieces + 1:
            receive(2)
    receive(3)
    result_copy(2).start()

    high, low = split(jnp.broadcast_to(weight[...].reshape(1, size), (16, size)))
    part = [multiply(high, low, h)[:8] for h in range(2)]
    shares[me] = jnp.where(left(part[0].shape), part[0], part[1])

    for j in range(1, n):
        pltpu.make_async_remote_copy(
            src_ref=shares.at[me], dst_ref=shares.at[me], send_sem=o_send,
            recv_sem=o_recv, device_id={"rows": lax.rem(me + j, n)}).start()

    @pl.when(is_hub)
    def _():
        await_bytes(names.at[pl.ds(0, hubs - 1)], n_send)
        for p in range(4):
            await_bytes(send1.at[p, :, :, pl.ds(0, packed - rows), :], s1_send.at[p])
            await_bytes(send3.at[p, :, pl.ds(0, half - 1)], s3_send.at[p])
            for c in range(pieces):
                second(p, c).wait_send()

    @pl.when(jnp.logical_not(is_hub))
    def _():
        await_bytes(names.at[pl.ds(0, hubs)], n_send)
        for p in range(4):
            await_bytes(send1.at[p], s1_send.at[p])

    await_bytes(shares.at[pl.ds(0, n - 1)], o_send)
    await_bytes(shares.at[pl.ds(0, n - 1)], o_recv)
    total = shares[0]
    for other in range(1, n):
        total = total + shares[other]
    observed[...] = total[:1]
    for level in range(3):
        result_copy(level).wait()


def body(rhs, diag_inv, tiles, dest, obs_weight):
    n = lax.axis_size("rows")
    size, width = rhs.shape[1], rhs.shape[2]
    half, hubs = n // 2, n // 4
    pieces = PIECES
    packed = size // pieces // 2
    rows = packed // hubs
    f32, bf16 = jnp.float32, jnp.bfloat16
    dma = pltpu.SemaphoreType.DMA
    vmem = pl.BlockSpec(memory_space=pltpu.VMEM)
    anywhere = pl.BlockSpec(memory_space=pl.ANY)
    sol, observed = pl.pallas_call(
        functools.partial(kernel, n, pieces),
        out_shape=(
            jax.ShapeDtypeStruct((3, size, width), f32),
            jax.ShapeDtypeStruct((1, width), f32),
        ),
        in_specs=[anywhere, vmem, pl.BlockSpec(memory_space=pltpu.SMEM), anywhere, anywhere],
        out_specs=(anywhere, vmem),
        scratch_shapes=[pltpu.VMEM((n + 1, rows, width), f32) for _ in range(4 * pieces)] + [
            pltpu.VMEM((3, size, width), f32),
            pltpu.VMEM((3, size, size), f32),
            pltpu.VMEM((2, 2, size, size), f32),
            pltpu.VMEM((3, size, size), bf16),
            pltpu.VMEM((3, size, size), bf16),
            pltpu.VMEM((2, 2, size, size), bf16),
            pltpu.VMEM((2, 2, size, size), bf16),
            pltpu.VMEM((2, size, 2 * width), bf16),
            pltpu.VMEM((2, size, width), f32),
            pltpu.VMEM((4, pieces, 2, packed, width), f32),
            pltpu.VMEM((4, pieces, half, rows, width), f32),
            pltpu.VMEM((4, pieces, half, rows, width), f32),
            pltpu.VMEM((2, half, rows, width), f32),
            pltpu.VMEM((4, pieces, half, rows, width), f32),
            pltpu.VMEM((4, pieces, packed, width), f32),
            pltpu.VMEM((8, 128), jnp.int32),
            pltpu.VMEM((half, 8, 128), jnp.int32),
            pltpu.VMEM((n, 128), jnp.int32),
            pltpu.SMEM((n, 128), jnp.int32),
            pltpu.VMEM((n, 8, width), f32),
            dma((10,)), dma((3,)),
            dma((4,)), dma((4, pieces)),
            dma((4, pieces)), dma((4, pieces)),
            dma((4,)), dma((4,)),
            dma, dma, dma, dma, dma,
        ],
        compiler_params=pltpu.CompilerParams(
            collective_id=0, has_side_effects=True, vmem_limit_bytes=60 * 1024 * 1024
        ),
        cost_estimate=pl.CostEstimate(
            flops=7 * 3 * 2 * size * size * width, bytes_accessed=7 * 4 * size * size, transcendentals=0
        ),
    )(rhs, obs_weight, dest.reshape(2, 2), diag_inv, tiles)
    return sol, observed.reshape(width)


def solution(mesh):
    in_specs = (
        P(None, "rows", "parts"),
        P(None, "rows", None),
        P(None, "rows", None, None),
        P(None, "rows", None),
        P("rows"),
    )
    out_specs = (P(None, "rows", "parts"), P("parts"))
    return jax.shard_map(body, mesh=mesh, in_specs=in_specs, out_specs=out_specs, check_vma=False)
```

```python
import functools
import math
import jax
import jax.numpy as jnp
from jax import lax
from jax.experimental import pallas as pl
from jax.experimental.pallas import tpu as pltpu
from jax.sharding import PartitionSpec as P

CAP = 4
PIECES = 3
OWN = 4


def split(value):
    high = value.astype(jnp.bfloat16)
    return high, (value - high.astype(jnp.float32)).astype(jnp.bfloat16)


def kernel(n, pieces, rhs, weight, dest, diag, tiles, sol, observed, *scratch):
    stage1 = [scratch[p * pieces : (p + 1) * pieces] for p in range(4)]
    (
        rhs_v, diag_f, tile_f, diag_hi, diag_lo, tile_hi, tile_lo, solved, sol_v,
        send1, send2, recv2, own, send3, update, share, names, places_v, table, shares,
        load_sem, out_sem, s1_send, s1_recv, s2_send, s2_recv, s3_send, s3_recv,
        n_send, n_recv, n_copy, o_send, o_recv,
    ) = scratch[4 * pieces :]
    size, width = rhs.shape[1], rhs.shape[2]
    half, hubs = n // 2, n // 4
    block = size // pieces
    packed = block // 2
    rows = packed // hubs
    me = lax.axis_index("rows")
    side = me // half
    base = side * half
    pos = me - base
    first_hub = (1 - side) * hubs
    is_hub = jnp.logical_and(pos >= first_hub, pos < first_hub + hubs)
    hub = pos - first_hub
    opposite = (1 - side) * half
    peer = me + hubs * (1 - 2 * side)

    barrier = pltpu.get_barrier_semaphore()
    for j in range(1, n):
        pl.semaphore_signal(barrier, inc=1, device_id={"rows": lax.rem(me + j, n)})

    def await_bytes(ref, sem):
        pltpu.make_async_copy(ref, ref, sem).wait()

    loads = []

    def load(source, target):
        loads.append(pltpu.make_async_copy(source, target, load_sem.at[len(loads)]))

    for level in range(3):
        load(rhs.at[level], rhs_v.at[level])
        load(diag.at[level], diag_f.at[level])
        if level < 2:
            for k in range(2):
                load(tiles.at[level, k], tile_f.at[level, k])
    for copy in loads[:4]:
        copy.start()

    strip = math.gcd(block, 64)

    def split_rows(source, high_ref, low_ref, start, count):
        def step(i, carry):
            at = pl.ds(pl.multiple_of(start + i * strip, strip), strip)
            high, low = split(source[at, :])
            high_ref[at, :] = high
            low_ref[at, :] = low
            return carry
        lax.fori_loop(0, count // strip, step, 0)

    def await_diag(level):
        loads[4 * level].wait()
        loads[4 * level + 1].wait()

    def split_diag(level, start, count):
        split_rows(diag_f.at[level], diag_hi.at[level], diag_lo.at[level], start, count)

    def await_tiles(level):
        for k in range(2):
            loads[4 * level + 2 + k].wait()

    def split_tiles(level, start, count):
        for k in range(2):
            split_rows(tile_f.at[level, k], tile_hi.at[level, k], tile_lo.at[level, k], start, count)

    def left(shape):
        return lax.broadcasted_iota(jnp.int32, shape, 1) < width // 2

    def swap(value):
        return pltpu.roll(value, width // 2, 1)

    def twice(value, h):
        low, high = (value, swap(value)) if h == 0 else (swap(value), value)
        return jnp.where(left(value.shape), low, high)

    def keep(h, value):
        high, low = split(value)
        mask = left(value.shape)
        both = jnp.where(mask, high.astype(jnp.float32), low.astype(jnp.float32))
        solved[h, :, :width] = both.astype(jnp.bfloat16)
        solved[h, :, width:] = high

    def multiply(high, low, h):
        wide = jnp.dot(high, solved[h, :, :width], preferred_element_type=jnp.float32)
        return wide + swap(wide) + jnp.dot(low, solved[h, :, width:], preferred_element_type=jnp.float32)

    def solve(level, h, current):
        keep(h, current)
        for c in range(pieces):
            at = pl.ds(c * block, block)
            sol_v[h, at, :] = multiply(diag_hi[level, at, :], diag_lo[level, at, :], h)
        value = sol_v[h]
        keep(h, value)
        if h == 0:
            mixed = jnp.where(left(value.shape), value, rhs_v[level])
        else:
            mixed = jnp.where(left(value.shape), rhs_v[level], value)
        rhs_v[level] = mixed

    def result_copy(level):
        return pltpu.make_async_copy(rhs_v.at[level], sol.at[level], out_sem.at[level])

    def names_copy(to):
        return pltpu.make_async_remote_copy(
            src_ref=share, dst_ref=names.at[pos], send_sem=n_send, recv_sem=n_recv,
            device_id={"rows": base + first_hub + to})

    def first(p, c, to):
        return pltpu.make_async_remote_copy(
            src_ref=send1.at[p, c, :, pl.ds(pl.multiple_of(to * rows, rows), rows), :],
            dst_ref=stage1[p][c].at[pl.ds(2 * pos, 2)],
            send_sem=s1_send.at[p], recv_sem=s1_recv.at[p, c],
            device_id={"rows": base + first_hub + to})

    def second(p, c):
        return pltpu.make_async_remote_copy(
            src_ref=send2.at[p, c], dst_ref=recv2.at[p, c],
            send_sem=s2_send.at[p, c], recv_sem=s2_recv.at[p, c], device_id={"rows": peer})

    def third(p, c, owner):
        at = pl.ds(pl.multiple_of(hub * rows, rows), rows)
        return pltpu.make_async_remote_copy(
            src_ref=send3.at[p, c, owner], dst_ref=update.at[p, c, at, :],
            send_sem=s3_send.at[p], recv_sem=s3_recv.at[p],
            device_id={"rows": base + owner})

    def send_products(p):
        t, h = p // 2, p % 2
        for c in range(pieces):
            if p == 0:
                split_tiles(0, c * block, block)
            at = pl.ds(c * block, block)
            for k in range(2):
                value = multiply(tile_hi[t, k, at, :], tile_lo[t, k, at, :], h)
                top, bottom = value[:packed], value[packed:]
                send1[p, c, k] = jnp.where(left(top.shape), top, bottom)
            @pl.when(is_hub)
            def _():
                at = pl.ds(pl.multiple_of(hub * rows, rows), rows)
                stage1[p][c][pl.ds(2 * pos, 2)] = send1[p, c, :, at, :]

            @pl.when(jnp.logical_not(is_hub))
            def _():
                first(p, c, lax.rem(pos, hubs)).start()

            for j in range(1, hubs):
                first(p, c, lax.rem(pos + j, hubs)).start()

    def build_table():
        await_bytes(names.at[pl.ds(0, half - 1)], n_recv)
        shape = places_v.shape
        target = lax.broadcasted_iota(jnp.int32, shape, 0)
        turn = lax.broadcasted_iota(jnp.int32, shape, 1) % CAP
        count = jnp.zeros(shape, jnp.int32)
        place = jnp.full(shape, n, jnp.int32)
        for q in range(n):
            hit = jnp.broadcast_to(names[q // 2, q % 2 : q % 2 + 1, :], shape) == target
            place = jnp.where(jnp.logical_and(hit, count == turn), q, place)
            count = count + jnp.where(hit, 1, 0)
        places_v[...] = place
        move = pltpu.make_async_copy(places_v, table, n_copy)
        move.start()
        move.wait()

    def add_up(p, c, start, out):
        buffer, column = stage1[p][c], p // 2 * CAP

        for i in range(half):
            d = start + i
            total = buffer[table[d, column]] + buffer[table[d, column + 1]]
            out[i] = total + (buffer[table[d, column + 2]] + buffer[table[d, column + 3]])

    def give_back(step):
        @pl.when(is_hub)
        def _():
            finish(step)

    def finish(step):
        p, c = step // pieces, step % pieces
        second(p, c).wait_recv()

        for i in range(half):
            send3[p, c, i] = own[step % OWN, i] + recv2[p, c, i]
        for j in range(1, half):
            third(p, c, lax.rem(pos + j, half)).start()
        update[p, c, pl.ds(pl.multiple_of(hub * rows, rows), rows), :] = send3[p, c, pos]

    def gather(step):
        p, c = step // pieces, step % pieces

        @pl.when(is_hub)
        def _():
            if step == 0:
                build_table()
            await_bytes(stage1[p][c].at[pl.ds(0, 2 * (half - 1))], s1_recv.at[p, c])
            add_up(p, c, opposite, send2.at[p, c])
            second(p, c).start()
            add_up(p, c, base, own.at[step % OWN])

    def receive(p):
        t, h = p // 2, p % 2
        @pl.when(is_hub)
        def _():
            await_bytes(update.at[p, :, pl.ds(0, packed - rows), :], s3_recv.at[p])

        @pl.when(jnp.logical_not(is_hub))
        def _():
            await_bytes(update.at[p], s3_recv.at[p])

        parts = []
        for c in range(pieces):
            value = update[p, c]
            parts += [twice(value, 0), twice(value, 1)]
        solve(t + 1, h, twice(rhs_v[t + 1], h) - jnp.concatenate(parts, axis=0))

    line = lax.broadcasted_iota(jnp.int32, share.shape, 0)
    lane = lax.broadcasted_iota(jnp.int32, share.shape, 1)
    value = jnp.zeros(share.shape, jnp.int32)
    for k in range(2):
        value = jnp.where(line == k, jnp.where(lane < CAP, dest[0, k], dest[1, k]), value)
    share[...] = value
    for p in range(4):
        for c in range(pieces):
            stage1[p][c][n] = jnp.zeros((rows, width), jnp.float32)

    await_diag(0)
    split_diag(0, 0, size)
    solve(0, 0, twice(rhs_v[0], 0))
    pl.semaphore_wait(barrier, n - 1)
    @pl.when(is_hub)
    def _():
        names[pos] = share[...]

    @pl.when(jnp.logical_not(is_hub))
    def _():
        names_copy(lax.rem(pos, hubs)).start()

    for j in range(1, hubs):
        names_copy(lax.rem(pos + j, hubs)).start()
    await_tiles(0)
    for copy in loads[4:]:
        copy.start()
    send_products(0)
    solve(0, 1, twice(rhs_v[0], 1))
    result_copy(0).start()
    send_products(1)

    gather(0)
    await_diag(1)
    split_diag(1, 0, size)
    await_tiles(1)
    split_tiles(1, 0, size)
    for step in range(1, pieces + 1):
        gather(step)
        give_back(step - 1)
    for step in range(pieces + 1, 2 * pieces):
        gather(step)
        if step < 2 * pieces - 1:
            give_back(step - 1)
    receive(0)
    send_products(2)
    for step in range(2 * pieces - 2, 2 * pieces):
        give_back(step)
    await_diag(2)
    split_diag(2, 0, size)
    gather(2 * pieces)
    receive(1)
    result_copy(1).start()
    send_products(3)
    for step in range(2 * pieces + 1, 3 * pieces + 1):
        gather(step)
        give_back(step - 1)
    for step in range(3 * pieces + 1, 4 * pieces):
        gather(step)
        if step < 4 * pieces - 1:
            give_back(step - 1)
    receive(2)
    for step in range(4 * pieces - 2, 4 * pieces):
        give_back(step)
    receive(3)
    result_copy(2).start()

    high, low = split(jnp.broadcast_to(weight[...].reshape(1, size), (16, size)))
    part = [multiply(high, low, h)[:8] for h in range(2)]
    shares[me] = jnp.where(left(part[0].shape), part[0], part[1])

    for j in range(1, n):
        pltpu.make_async_remote_copy(
            src_ref=shares.at[me], dst_ref=shares.at[me], send_sem=o_send,
            recv_sem=o_recv, device_id={"rows": lax.rem(me + j, n)}).start()

    @pl.when(is_hub)
    def _():
        await_bytes(names.at[pl.ds(0, hubs - 1)], n_send)
        for p in range(4):
            await_bytes(send1.at[p, :, :, pl.ds(0, packed - rows), :], s1_send.at[p])
            await_bytes(send3.at[p, :, pl.ds(0, half - 1)], s3_send.at[p])
            for c in range(pieces):
                second(p, c).wait_send()

    @pl.when(jnp.logical_not(is_hub))
    def _():
        await_bytes(names.at[pl.ds(0, hubs)], n_send)
        for p in range(4):
            await_bytes(send1.at[p], s1_send.at[p])

    await_bytes(shares.at[pl.ds(0, n - 1)], o_send)
    await_bytes(shares.at[pl.ds(0, n - 1)], o_recv)
    total = shares[0]
    for other in range(1, n):
        total = total + shares[other]
    observed[...] = total[:1]
    for level in range(3):
        result_copy(level).wait()


def body(rhs, diag_inv, tiles, dest, obs_weight):
    n = lax.axis_size("rows")
    size, width = rhs.shape[1], rhs.shape[2]
    half, hubs = n // 2, n // 4
    pieces = PIECES
    packed = size // pieces // 2
    rows = packed // hubs
    f32, bf16 = jnp.float32, jnp.bfloat16
    dma = pltpu.SemaphoreType.DMA
    vmem = pl.BlockSpec(memory_space=pltpu.VMEM)
    anywhere = pl.BlockSpec(memory_space=pl.ANY)
    sol, observed = pl.pallas_call(
        functools.partial(kernel, n, pieces),
        out_shape=(
            jax.ShapeDtypeStruct((3, size, width), f32),
            jax.ShapeDtypeStruct((1, width), f32),
        ),
        in_specs=[anywhere, vmem, pl.BlockSpec(memory_space=pltpu.SMEM), anywhere, anywhere],
        out_specs=(anywhere, vmem),
        scratch_shapes=[pltpu.VMEM((n + 1, rows, width), f32) for _ in range(4 * pieces)] + [
            pltpu.VMEM((3, size, width), f32),
            pltpu.VMEM((3, size, size), f32),
            pltpu.VMEM((2, 2, size, size), f32),
            pltpu.VMEM((3, size, size), bf16),
            pltpu.VMEM((3, size, size), bf16),
            pltpu.VMEM((2, 2, size, size), bf16),
            pltpu.VMEM((2, 2, size, size), bf16),
            pltpu.VMEM((2, size, 2 * width), bf16),
            pltpu.VMEM((2, size, width), f32),
            pltpu.VMEM((4, pieces, 2, packed, width), f32),
            pltpu.VMEM((4, pieces, half, rows, width), f32),
            pltpu.VMEM((4, pieces, half, rows, width), f32),
            pltpu.VMEM((OWN, half, rows, width), f32),
            pltpu.VMEM((4, pieces, half, rows, width), f32),
            pltpu.VMEM((4, pieces, packed, width), f32),
            pltpu.VMEM((8, 128), jnp.int32),
            pltpu.VMEM((half, 8, 128), jnp.int32),
            pltpu.VMEM((n, 128), jnp.int32),
            pltpu.SMEM((n, 128), jnp.int32),
            pltpu.VMEM((n, 8, width), f32),
            dma((10,)), dma((3,)),
            dma((4,)), dma((4, pieces)),
            dma((4, pieces)), dma((4, pieces)),
            dma((4,)), dma((4,)),
            dma, dma, dma, dma, dma,
        ],
        compiler_params=pltpu.CompilerParams(
            collective_id=0, has_side_effects=True, vmem_limit_bytes=60 * 1024 * 1024
        ),
        cost_estimate=pl.CostEstimate(
            flops=7 * 3 * 2 * size * size * width, bytes_accessed=7 * 4 * size * size, transcendentals=0
        ),
    )(rhs, obs_weight, dest.reshape(2, 2), diag_inv, tiles)
    return sol, observed.reshape(width)


def solution(mesh):
    in_specs = (
        P(None, "rows", "parts"),
        P(None, "rows", None),
        P(None, "rows", None, None),
        P(None, "rows", None),
        P("rows"),
    )
    out_specs = (P(None, "rows", "parts"), P("parts"))
    return jax.shard_map(body, mesh=mesh, in_specs=in_specs, out_specs=out_specs, check_vma=False)
```

```python
import functools
import math
import jax
import jax.numpy as jnp
from jax import lax
from jax.experimental import pallas as pl
from jax.experimental.pallas import tpu as pltpu
from jax.sharding import PartitionSpec as P

CAP = 4
PIECES = 3
OWN = 4


def split(value):
    high = value.astype(jnp.bfloat16)
    return high, (value - high.astype(jnp.float32)).astype(jnp.bfloat16)


def kernel(n, pieces, rhs, weight, dest, diag, tiles, sol, observed, *scratch):
    stage1 = [scratch[p * pieces : (p + 1) * pieces] for p in range(4)]
    (
        rhs_v, diag_f, tile_f, diag_hi, diag_lo, tile_hi, tile_lo, solved, sol_v,
        send1, send2, recv2, own, send3, update, share, names, places_v, table, shares,
        load_sem, out_sem, s1_send, s1_recv, s2_send, s2_recv, s3_send, s3_recv,
        n_send, n_recv, n_copy, o_send, o_recv,
    ) = scratch[4 * pieces :]
    size, width = rhs.shape[1], rhs.shape[2]
    half = n // 2
    block = size // pieces
    packed = block // 2
    rows = packed // half
    me = lax.axis_index("rows")
    side = me // half
    base = side * half
    pos = me - base
    opposite = (1 - side) * half
    peer = me + half * (1 - 2 * side)

    barrier = pltpu.get_barrier_semaphore()
    for j in range(1, n):
        pl.semaphore_signal(barrier, inc=1, device_id={"rows": lax.rem(me + j, n)})

    def await_bytes(ref, sem):
        pltpu.make_async_copy(ref, ref, sem).wait()

    loads = []

    def load(source, target):
        loads.append(pltpu.make_async_copy(source, target, load_sem.at[len(loads)]))

    for level in range(3):
        load(rhs.at[level], rhs_v.at[level])
        load(diag.at[level], diag_f.at[level])
        if level < 2:
            for k in range(2):
                load(tiles.at[level, k], tile_f.at[level, k])
    for copy in loads[:4]:
        copy.start()

    strip = math.gcd(block, 64)

    def split_rows(source, high_ref, low_ref, start, count):
        def step(i, carry):
            at = pl.ds(pl.multiple_of(start + i * strip, strip), strip)
            high, low = split(source[at, :])
            high_ref[at, :] = high
            low_ref[at, :] = low
            return carry
        lax.fori_loop(0, count // strip, step, 0)

    def await_diag(level):
        loads[4 * level].wait()
        loads[4 * level + 1].wait()

    def split_diag(level, start, count):
        split_rows(diag_f.at[level], diag_hi.at[level], diag_lo.at[level], start, count)

    def await_tiles(level):
        for k in range(2):
            loads[4 * level + 2 + k].wait()

    def split_tiles(level, start, count):
        for k in range(2):
            split_rows(tile_f.at[level, k], tile_hi.at[level, k], tile_lo.at[level, k], start, count)

    def left(shape):
        return lax.broadcasted_iota(jnp.int32, shape, 1) < width // 2

    def swap(value):
        return pltpu.roll(value, width // 2, 1)

    def twice(value, h):
        low, high = (value, swap(value)) if h == 0 else (swap(value), value)
        return jnp.where(left(value.shape), low, high)

    def keep(h, value):
        high, low = split(value)
        mask = left(value.shape)
        both = jnp.where(mask, high.astype(jnp.float32), low.astype(jnp.float32))
        solved[h, :, :width] = both.astype(jnp.bfloat16)
        solved[h, :, width:] = high

    def multiply(high, low, h):
        wide = jnp.dot(high, solved[h, :, :width], preferred_element_type=jnp.float32)
        return wide + swap(wide) + jnp.dot(low, solved[h, :, width:], preferred_element_type=jnp.float32)

    def solve(level, h, current):
        keep(h, current)
        for c in range(pieces):
            at = pl.ds(c * block, block)
            sol_v[h, at, :] = multiply(diag_hi[level, at, :], diag_lo[level, at, :], h)
        value = sol_v[h]
        keep(h, value)
        if h == 0:
            mixed = jnp.where(left(value.shape), value, rhs_v[level])
        else:
            mixed = jnp.where(left(value.shape), rhs_v[level], value)
        rhs_v[level] = mixed

    def result_copy(level):
        return pltpu.make_async_copy(rhs_v.at[level], sol.at[level], out_sem.at[level])

    def names_copy(to):
        return pltpu.make_async_remote_copy(
            src_ref=share, dst_ref=names.at[pos], send_sem=n_send, recv_sem=n_recv,
            device_id={"rows": base + to})

    def first(p, c, to):
        return pltpu.make_async_remote_copy(
            src_ref=send1.at[p, c, :, pl.ds(pl.multiple_of(to * rows, rows), rows), :],
            dst_ref=stage1[p][c].at[pl.ds(2 * pos, 2)],
            send_sem=s1_send.at[p], recv_sem=s1_recv.at[p, c],
            device_id={"rows": base + to})

    def second(p, c):
        return pltpu.make_async_remote_copy(
            src_ref=send2.at[p, c], dst_ref=recv2.at[p, c],
            send_sem=s2_send.at[p, c], recv_sem=s2_recv.at[p, c], device_id={"rows": peer})

    def third(p, c, owner):
        at = pl.ds(pl.multiple_of(pos * rows, rows), rows)
        return pltpu.make_async_remote_copy(
            src_ref=send3.at[p, c, owner], dst_ref=update.at[p, c, at, :],
            send_sem=s3_send.at[p], recv_sem=s3_recv.at[p],
            device_id={"rows": base + owner})

    def send_products(p):
        t, h = p // 2, p % 2
        for c in range(pieces):
            if p == 0:
                split_tiles(0, c * block, block)
            at = pl.ds(c * block, block)
            for k in range(2):
                value = multiply(tile_hi[t, k, at, :], tile_lo[t, k, at, :], h)
                top, bottom = value[:packed], value[packed:]
                send1[p, c, k] = jnp.where(left(top.shape), top, bottom)
            at = pl.ds(pl.multiple_of(pos * rows, rows), rows)
            stage1[p][c][pl.ds(2 * pos, 2)] = send1[p, c, :, at, :]


            for j in range(1, half):
                first(p, c, lax.rem(pos + j, half)).start()

    def build_table():
        await_bytes(names.at[pl.ds(0, half - 1)], n_recv)
        shape = places_v.shape
        target = lax.broadcasted_iota(jnp.int32, shape, 0)
        turn = lax.broadcasted_iota(jnp.int32, shape, 1) % CAP
        count = jnp.zeros(shape, jnp.int32)
        place = jnp.full(shape, n, jnp.int32)
        for q in range(n):
            hit = jnp.broadcast_to(names[q // 2, q % 2 : q % 2 + 1, :], shape) == target
            place = jnp.where(jnp.logical_and(hit, count == turn), q, place)
            count = count + jnp.where(hit, 1, 0)
        places_v[...] = place
        move = pltpu.make_async_copy(places_v, table, n_copy)
        move.start()
        move.wait()

    def add_up(p, c, start, out):
        buffer, column = stage1[p][c], p // 2 * CAP

        for i in range(half):
            d = start + i
            total = buffer[table[d, column]] + buffer[table[d, column + 1]]
            out[i] = total + (buffer[table[d, column + 2]] + buffer[table[d, column + 3]])

    def give_back(step):
        finish(step)

    def finish(step):
        p, c = step // pieces, step % pieces
        second(p, c).wait_recv()

        for i in range(half):
            send3[p, c, i] = own[step % OWN, i] + recv2[p, c, i]
        for j in range(1, half):
            third(p, c, lax.rem(pos + j, half)).start()
        update[p, c, pl.ds(pl.multiple_of(pos * rows, rows), rows), :] = send3[p, c, pos]

    def gather(step):
        p, c = step // pieces, step % pieces

        if step == 0:
            build_table()
        await_bytes(stage1[p][c].at[pl.ds(0, 2 * (half - 1))], s1_recv.at[p, c])
        add_up(p, c, opposite, send2.at[p, c])
        second(p, c).start()
        add_up(p, c, base, own.at[step % OWN])

    def receive(p):
        t, h = p // 2, p % 2
        await_bytes(update.at[p, :, pl.ds(0, packed - rows), :], s3_recv.at[p])


        parts = []
        for c in range(pieces):
            value = update[p, c]
            parts += [twice(value, 0), twice(value, 1)]
        solve(t + 1, h, twice(rhs_v[t + 1], h) - jnp.concatenate(parts, axis=0))

    line = lax.broadcasted_iota(jnp.int32, share.shape, 0)
    lane = lax.broadcasted_iota(jnp.int32, share.shape, 1)
    value = jnp.zeros(share.shape, jnp.int32)
    for k in range(2):
        value = jnp.where(line == k, jnp.where(lane < CAP, dest[0, k], dest[1, k]), value)
    share[...] = value
    for p in range(4):
        for c in range(pieces):
            stage1[p][c][n] = jnp.zeros((rows, width), jnp.float32)

    await_diag(0)
    split_diag(0, 0, size)
    solve(0, 0, twice(rhs_v[0], 0))
    pl.semaphore_wait(barrier, n - 1)
    names[pos] = share[...]


    for j in range(1, half):
        names_copy(lax.rem(pos + j, half)).start()
    await_tiles(0)
    for copy in loads[4:]:
        copy.start()
    send_products(0)
    solve(0, 1, twice(rhs_v[0], 1))
    result_copy(0).start()
    send_products(1)

    gather(0)
    await_diag(1)
    split_diag(1, 0, size)
    await_tiles(1)
    split_tiles(1, 0, size)
    for step in range(1, pieces + 1):
        gather(step)
        give_back(step - 1)
    for step in range(pieces + 1, 2 * pieces):
        gather(step)
        if step < 2 * pieces - 1:
            give_back(step - 1)
    receive(0)
    send_products(2)
    for step in range(2 * pieces - 2, 2 * pieces):
        give_back(step)
    await_diag(2)
    split_diag(2, 0, size)
    gather(2 * pieces)
    receive(1)
    result_copy(1).start()
    send_products(3)
    for step in range(2 * pieces + 1, 3 * pieces + 1):
        gather(step)
        give_back(step - 1)
    for step in range(3 * pieces + 1, 4 * pieces):
        gather(step)
        if step < 4 * pieces - 1:
            give_back(step - 1)
    receive(2)
    for step in range(4 * pieces - 2, 4 * pieces):
        give_back(step)
    receive(3)
    result_copy(2).start()

    high, low = split(jnp.broadcast_to(weight[...].reshape(1, size), (16, size)))
    part = [multiply(high, low, h)[:8] for h in range(2)]
    shares[me] = jnp.where(left(part[0].shape), part[0], part[1])

    for j in range(1, n):
        pltpu.make_async_remote_copy(
            src_ref=shares.at[me], dst_ref=shares.at[me], send_sem=o_send,
            recv_sem=o_recv, device_id={"rows": lax.rem(me + j, n)}).start()

    await_bytes(names.at[pl.ds(0, half - 1)], n_send)
    for p in range(4):
        await_bytes(send1.at[p, :, :, pl.ds(0, packed - rows), :], s1_send.at[p])
        await_bytes(send3.at[p, :, pl.ds(0, half - 1)], s3_send.at[p])
        for c in range(pieces):
            second(p, c).wait_send()

    await_bytes(shares.at[pl.ds(0, n - 1)], o_send)
    await_bytes(shares.at[pl.ds(0, n - 1)], o_recv)
    total = shares[0]
    for other in range(1, n):
        total = total + shares[other]
    observed[...] = total[:1]
    for level in range(3):
        result_copy(level).wait()


def body(rhs, diag_inv, tiles, dest, obs_weight):
    n = lax.axis_size("rows")
    size, width = rhs.shape[1], rhs.shape[2]
    half = n // 2
    pieces = PIECES
    packed = size // pieces // 2
    rows = packed // half
    f32, bf16 = jnp.float32, jnp.bfloat16
    dma = pltpu.SemaphoreType.DMA
    vmem = pl.BlockSpec(memory_space=pltpu.VMEM)
    anywhere = pl.BlockSpec(memory_space=pl.ANY)
    sol, observed = pl.pallas_call(
        functools.partial(kernel, n, pieces),
        out_shape=(
            jax.ShapeDtypeStruct((3, size, width), f32),
            jax.ShapeDtypeStruct((1, width), f32),
        ),
        in_specs=[anywhere, vmem, pl.BlockSpec(memory_space=pltpu.SMEM), anywhere, anywhere],
        out_specs=(anywhere, vmem),
        scratch_shapes=[pltpu.VMEM((n + 1, rows, width), f32) for _ in range(4 * pieces)] + [
            pltpu.VMEM((3, size, width), f32),
            pltpu.VMEM((3, size, size), f32),
            pltpu.VMEM((2, 2, size, size), f32),
            pltpu.VMEM((3, size, size), bf16),
            pltpu.VMEM((3, size, size), bf16),
            pltpu.VMEM((2, 2, size, size), bf16),
            pltpu.VMEM((2, 2, size, size), bf16),
            pltpu.VMEM((2, size, 2 * width), bf16),
            pltpu.VMEM((2, size, width), f32),
            pltpu.VMEM((4, pieces, 2, packed, width), f32),
            pltpu.VMEM((4, pieces, half, rows, width), f32),
            pltpu.VMEM((4, pieces, half, rows, width), f32),
            pltpu.VMEM((OWN, half, rows, width), f32),
            pltpu.VMEM((4, pieces, half, rows, width), f32),
            pltpu.VMEM((4, pieces, packed, width), f32),
            pltpu.VMEM((8, 128), jnp.int32),
            pltpu.VMEM((half, 8, 128), jnp.int32),
            pltpu.VMEM((n, 128), jnp.int32),
            pltpu.SMEM((n, 128), jnp.int32),
            pltpu.VMEM((n, 8, width), f32),
            dma((10,)), dma((3,)),
            dma((4,)), dma((4, pieces)),
            dma((4, pieces)), dma((4, pieces)),
            dma((4,)), dma((4,)),
            dma, dma, dma, dma, dma,
        ],
        compiler_params=pltpu.CompilerParams(
            collective_id=0, has_side_effects=True, vmem_limit_bytes=60 * 1024 * 1024
        ),
        cost_estimate=pl.CostEstimate(
            flops=7 * 3 * 2 * size * size * width, bytes_accessed=7 * 4 * size * size, transcendentals=0
        ),
    )(rhs, obs_weight, dest.reshape(2, 2), diag_inv, tiles)
    return sol, observed.reshape(width)


def solution(mesh):
    in_specs = (
        P(None, "rows", "parts"),
        P(None, "rows", None),
        P(None, "rows", None, None),
        P(None, "rows", None),
        P("rows"),
    )
    out_specs = (P(None, "rows", "parts"), P("parts"))
    return jax.shard_map(body, mesh=mesh, in_specs=in_specs, out_specs=out_specs, check_vma=False)
```

```python
import functools
import math
import jax
import jax.numpy as jnp
from jax import lax
from jax.experimental import pallas as pl
from jax.experimental.pallas import tpu as pltpu
from jax.sharding import PartitionSpec as P

CAP = 4
PIECES = 6


def split(value):
    high = value.astype(jnp.bfloat16)
    return high, (value - high.astype(jnp.float32)).astype(jnp.bfloat16)


def order_of_work(pieces):
    span = 8.0
    begin, events = [0.0, span], []
    for p in range(4):
        for c in range(pieces):
            at = begin[p] + (c + 1) * span / pieces
            events.append((at, "gather", p * pieces + c))
            events.append((at + 3.5, "return", p * pieces + c))
        ready = begin[p] + span + 6.5
        events.append((ready, "solve", p))
        if p < 2:
            begin.append(max(ready + 3.0, begin[-1] + span))
    return [event[1:] for event in sorted(events)]


def kernel(n, pieces, rhs, weight, dest, diag, tiles, sol, observed, *scratch):
    stage1 = [scratch[p * pieces : (p + 1) * pieces] for p in range(4)]
    (
        rhs_v, diag_f, tile_f, diag_hi, diag_lo, tile_hi, tile_lo, solved, sol_v,
        send1, send2, recv2, own, send3, update, share, names, places_v, table, shares,
        load_sem, out_sem, s1_send, s1_recv, s2_send, s2_recv, s3_send, s3_recv,
        n_send, n_recv, n_copy, o_send, o_recv,
    ) = scratch[4 * pieces :]
    size, width = rhs.shape[1], rhs.shape[2]
    half, hubs = n // 2, n // 4
    block = size // pieces
    packed = block // 2
    rows = packed // hubs
    me = lax.axis_index("rows")
    side = me // half
    base = side * half
    pos = me - base
    first_hub = (1 - side) * hubs
    is_hub = jnp.logical_and(pos >= first_hub, pos < first_hub + hubs)
    hub = pos - first_hub
    opposite = (1 - side) * half
    peer = me + hubs * (1 - 2 * side)

    barrier = pltpu.get_barrier_semaphore()
    for j in range(1, n):
        pl.semaphore_signal(barrier, inc=1, device_id={"rows": lax.rem(me + j, n)})

    def await_bytes(ref, sem):
        pltpu.make_async_copy(ref, ref, sem).wait()

    loads = []

    def load(source, target):
        loads.append(pltpu.make_async_copy(source, target, load_sem.at[len(loads)]))

    for level in range(3):
        load(rhs.at[level], rhs_v.at[level])
        load(diag.at[level], diag_f.at[level])
        if level < 2:
            for k in range(2):
                load(tiles.at[level, k], tile_f.at[level, k])
    for copy in loads[:4]:
        copy.start()

    strip = math.gcd(block, 64)

    def split_rows(source, high_ref, low_ref, start, count):
        def step(i, carry):
            at = pl.ds(pl.multiple_of(start + i * strip, strip), strip)
            high, low = split(source[at, :])
            high_ref[at, :] = high
            low_ref[at, :] = low
            return carry
        lax.fori_loop(0, count // strip, step, 0)

    def await_diag(level):
        loads[4 * level].wait()
        loads[4 * level + 1].wait()

    def split_diag(level, start, count):
        split_rows(diag_f.at[level], diag_hi.at[level], diag_lo.at[level], start, count)

    def await_tiles(level):
        for k in range(2):
            loads[4 * level + 2 + k].wait()

    def split_tiles(level, start, count):
        for k in range(2):
            split_rows(tile_f.at[level, k], tile_hi.at[level, k], tile_lo.at[level, k], start, count)

    def left(shape):
        return lax.broadcasted_iota(jnp.int32, shape, 1) < width // 2

    def swap(value):
        return pltpu.roll(value, width // 2, 1)

    def twice(value, h):
        low, high = (value, swap(value)) if h == 0 else (swap(value), value)
        return jnp.where(left(value.shape), low, high)

    def keep(h, value):
        high, low = split(value)
        mask = left(value.shape)
        both = jnp.where(mask, high.astype(jnp.float32), low.astype(jnp.float32))
        solved[h, :, :width] = both.astype(jnp.bfloat16)
        solved[h, :, width:] = high

    def multiply(high, low, h):
        wide = jnp.dot(high, solved[h, :, :width], preferred_element_type=jnp.float32)
        return wide + swap(wide) + jnp.dot(low, solved[h, :, width:], preferred_element_type=jnp.float32)

    def solve(level, h, current):
        keep(h, current)
        for c in range(pieces):
            at = pl.ds(c * block, block)
            sol_v[h, at, :] = multiply(diag_hi[level, at, :], diag_lo[level, at, :], h)
        value = sol_v[h]
        keep(h, value)
        if h == 0:
            mixed = jnp.where(left(value.shape), value, rhs_v[level])
        else:
            mixed = jnp.where(left(value.shape), rhs_v[level], value)
        rhs_v[level] = mixed

    def result_copy(level):
        return pltpu.make_async_copy(rhs_v.at[level], sol.at[level], out_sem.at[level])

    def names_copy(to):
        return pltpu.make_async_remote_copy(
            src_ref=share, dst_ref=names.at[pos], send_sem=n_send, recv_sem=n_recv,
            device_id={"rows": base + first_hub + to})

    def first(p, c, to):
        return pltpu.make_async_remote_copy(
            src_ref=send1.at[p, c, :, pl.ds(pl.multiple_of(to * rows, rows), rows), :],
            dst_ref=stage1[p][c].at[pl.ds(2 * pos, 2)],
            send_sem=s1_send.at[p], recv_sem=s1_recv.at[p, c],
            device_id={"rows": base + first_hub + to})

    def second(p, c):
        return pltpu.make_async_remote_copy(
            src_ref=send2.at[p, c], dst_ref=recv2.at[p, c],
            send_sem=s2_send.at[p, c], recv_sem=s2_recv.at[p, c], device_id={"rows": peer})

    def third(p, c, owner):
        at = pl.ds(pl.multiple_of(hub * rows, rows), rows)
        return pltpu.make_async_remote_copy(
            src_ref=send3.at[p, c, owner], dst_ref=update.at[p, c, at, :],
            send_sem=s3_send.at[p], recv_sem=s3_recv.at[p],
            device_id={"rows": base + owner})

    def send_products(p):
        t, h = p // 2, p % 2
        for c in range(pieces):
            if p == 0:
                split_tiles(0, c * block, block)
            at = pl.ds(c * block, block)
            for k in range(2):
                value = multiply(tile_hi[t, k, at, :], tile_lo[t, k, at, :], h)
                top, bottom = value[:packed], value[packed:]
                send1[p, c, k] = jnp.where(left(top.shape), top, bottom)
            @pl.when(is_hub)
            def _():
                at = pl.ds(pl.multiple_of(hub * rows, rows), rows)
                stage1[p][c][pl.ds(2 * pos, 2)] = send1[p, c, :, at, :]

            @pl.when(jnp.logical_not(is_hub))
            def _():
                first(p, c, lax.rem(pos, hubs)).start()

            for j in range(1, hubs):
                first(p, c, lax.rem(pos + j, hubs)).start()

    def build_table():
        await_bytes(names.at[pl.ds(0, half - 1)], n_recv)
        shape = places_v.shape
        target = lax.broadcasted_iota(jnp.int32, shape, 0)
        turn = lax.broadcasted_iota(jnp.int32, shape, 1) % CAP
        count = jnp.zeros(shape, jnp.int32)
        place = jnp.full(shape, n, jnp.int32)
        for q in range(n):
            hit = jnp.broadcast_to(names[q // 2, q % 2 : q % 2 + 1, :], shape) == target
            place = jnp.where(jnp.logical_and(hit, count == turn), q, place)
            count = count + jnp.where(hit, 1, 0)
        places_v[...] = place
        move = pltpu.make_async_copy(places_v, table, n_copy)
        move.start()
        move.wait()

    def add_up(p, c, start, out):
        buffer, column = stage1[p][c], p // 2 * CAP

        for i in range(half):
            d = start + i
            total = buffer[table[d, column]] + buffer[table[d, column + 1]]
            out[i] = total + (buffer[table[d, column + 2]] + buffer[table[d, column + 3]])

    def give_back(step):
        @pl.when(is_hub)
        def _():
            finish(step)

    def finish(step):
        p, c = step // pieces, step % pieces
        second(p, c).wait_recv()

        for i in range(half):
            send3[p, c, i] = own[step, i] + recv2[p, c, i]
        for j in range(1, half):
            third(p, c, lax.rem(pos + j, half)).start()
        update[p, c, pl.ds(pl.multiple_of(hub * rows, rows), rows), :] = send3[p, c, pos]

    def gather(step):
        p, c = step // pieces, step % pieces

        @pl.when(is_hub)
        def _():
            if step == 0:
                build_table()
            await_bytes(stage1[p][c].at[pl.ds(0, 2 * (half - 1))], s1_recv.at[p, c])
            add_up(p, c, opposite, send2.at[p, c])
            second(p, c).start()
            add_up(p, c, base, own.at[step])

    def receive(p):
        t, h = p // 2, p % 2
        @pl.when(is_hub)
        def _():
            await_bytes(update.at[p, :, pl.ds(0, packed - rows), :], s3_recv.at[p])

        @pl.when(jnp.logical_not(is_hub))
        def _():
            await_bytes(update.at[p], s3_recv.at[p])

        parts = []
        for c in range(pieces):
            value = update[p, c]
            parts += [twice(value, 0), twice(value, 1)]
        solve(t + 1, h, twice(rhs_v[t + 1], h) - jnp.concatenate(parts, axis=0))

    line = lax.broadcasted_iota(jnp.int32, share.shape, 0)
    lane = lax.broadcasted_iota(jnp.int32, share.shape, 1)
    value = jnp.zeros(share.shape, jnp.int32)
    for k in range(2):
        value = jnp.where(line == k, jnp.where(lane < CAP, dest[0, k], dest[1, k]), value)
    share[...] = value
    for p in range(4):
        for c in range(pieces):
            stage1[p][c][n] = jnp.zeros((rows, width), jnp.float32)

    await_diag(0)
    split_diag(0, 0, size)
    solve(0, 0, twice(rhs_v[0], 0))
    pl.semaphore_wait(barrier, n - 1)
    @pl.when(is_hub)
    def _():
        names[pos] = share[...]

    @pl.when(jnp.logical_not(is_hub))
    def _():
        names_copy(lax.rem(pos, hubs)).start()

    for j in range(1, hubs):
        names_copy(lax.rem(pos + j, hubs)).start()
    await_tiles(0)
    for copy in loads[4:]:
        copy.start()
    send_products(0)
    solve(0, 1, twice(rhs_v[0], 1))
    result_copy(0).start()
    send_products(1)

    for kind, item in order_of_work(pieces):
        if kind == "gather":
            gather(item)
            if item == 0:
                await_diag(1)
                split_diag(1, 0, size)
                await_tiles(1)
                split_tiles(1, 0, size)
            if item == 2 * pieces:
                await_diag(2)
                split_diag(2, 0, size)
        elif kind == "return":
            give_back(item)
        elif item < 3:
            receive(item)
            if item == 1:
                result_copy(1).start()
            if item < 2:
                send_products(item + 2)
    receive(3)
    result_copy(2).start()

    high, low = split(jnp.broadcast_to(weight[...].reshape(1, size), (16, size)))
    part = [multiply(high, low, h)[:8] for h in range(2)]
    shares[me] = jnp.where(left(part[0].shape), part[0], part[1])

    for j in range(1, n):
        pltpu.make_async_remote_copy(
            src_ref=shares.at[me], dst_ref=shares.at[me], send_sem=o_send,
            recv_sem=o_recv, device_id={"rows": lax.rem(me + j, n)}).start()

    @pl.when(is_hub)
    def _():
        await_bytes(names.at[pl.ds(0, hubs - 1)], n_send)
        for p in range(4):
            await_bytes(send1.at[p, :, :, pl.ds(0, packed - rows), :], s1_send.at[p])
            await_bytes(send3.at[p, :, pl.ds(0, half - 1)], s3_send.at[p])
            for c in range(pieces):
                second(p, c).wait_send()

    @pl.when(jnp.logical_not(is_hub))
    def _():
        await_bytes(names.at[pl.ds(0, hubs)], n_send)
        for p in range(4):
            await_bytes(send1.at[p], s1_send.at[p])

    await_bytes(shares.at[pl.ds(0, n - 1)], o_send)
    await_bytes(shares.at[pl.ds(0, n - 1)], o_recv)
    total = shares[0]
    for other in range(1, n):
        total = total + shares[other]
    observed[...] = total[:1]
    for level in range(3):
        result_copy(level).wait()


def body(rhs, diag_inv, tiles, dest, obs_weight):
    n = lax.axis_size("rows")
    size, width = rhs.shape[1], rhs.shape[2]
    half, hubs = n // 2, n // 4
    pieces = PIECES
    packed = size // pieces // 2
    rows = packed // hubs
    f32, bf16 = jnp.float32, jnp.bfloat16
    dma = pltpu.SemaphoreType.DMA
    vmem = pl.BlockSpec(memory_space=pltpu.VMEM)
    anywhere = pl.BlockSpec(memory_space=pl.ANY)
    sol, observed = pl.pallas_call(
        functools.partial(kernel, n, pieces),
        out_shape=(
            jax.ShapeDtypeStruct((3, size, width), f32),
            jax.ShapeDtypeStruct((1, width), f32),
        ),
        in_specs=[anywhere, vmem, pl.BlockSpec(memory_space=pltpu.SMEM), anywhere, anywhere],
        out_specs=(anywhere, vmem),
        scratch_shapes=[pltpu.VMEM((n + 1, rows, width), f32) for _ in range(4 * pieces)] + [
            pltpu.VMEM((3, size, width), f32),
            pltpu.VMEM((3, size, size), f32),
            pltpu.VMEM((2, 2, size, size), f32),
            pltpu.VMEM((3, size, size), bf16),
            pltpu.VMEM((3, size, size), bf16),
            pltpu.VMEM((2, 2, size, size), bf16),
            pltpu.VMEM((2, 2, size, size), bf16),
            pltpu.VMEM((2, size, 2 * width), bf16),
            pltpu.VMEM((2, size, width), f32),
            pltpu.VMEM((4, pieces, 2, packed, width), f32),
            pltpu.VMEM((4, pieces, half, rows, width), f32),
            pltpu.VMEM((4, pieces, half, rows, width), f32),
            pltpu.VMEM((4 * pieces, half, rows, width), f32),
            pltpu.VMEM((4, pieces, half, rows, width), f32),
            pltpu.VMEM((4, pieces, packed, width), f32),
            pltpu.VMEM((8, 128), jnp.int32),
            pltpu.VMEM((half, 8, 128), jnp.int32),
            pltpu.VMEM((n, 128), jnp.int32),
            pltpu.SMEM((n, 128), jnp.int32),
            pltpu.VMEM((n, 8, width), f32),
            dma((10,)), dma((3,)),
            dma((4,)), dma((4, pieces)),
            dma((4, pieces)), dma((4, pieces)),
            dma((4,)), dma((4,)),
            dma, dma, dma, dma, dma,
        ],
        compiler_params=pltpu.CompilerParams(
            collective_id=0, has_side_effects=True, vmem_limit_bytes=60 * 1024 * 1024
        ),
        cost_estimate=pl.CostEstimate(
            flops=7 * 3 * 2 * size * size * width, bytes_accessed=7 * 4 * size * size, transcendentals=0
        ),
    )(rhs, obs_weight, dest.reshape(2, 2), diag_inv, tiles)
    return sol, observed.reshape(width)


def solution(mesh):
    in_specs = (
        P(None, "rows", "parts"),
        P(None, "rows", None),
        P(None, "rows", None, None),
        P(None, "rows", None),
        P("rows"),
    )
    out_specs = (P(None, "rows", "parts"), P("parts"))
    return jax.shard_map(body, mesh=mesh, in_specs=in_specs, out_specs=out_specs, check_vma=False)
```

```python
import functools
import jax
import jax.numpy as jnp
from jax import lax
from jax.experimental import pallas as pl
from jax.experimental.pallas import tpu as pltpu
from jax.sharding import PartitionSpec as P

CAP = 4
PIECES = 3


def split(value):
    high = value.astype(jnp.bfloat16)
    return high, (value - high.astype(jnp.float32)).astype(jnp.bfloat16)


def kernel(n, pieces, rhs, weight, dest, diag, tiles, sol, observed, *scratch):
    stage1 = [scratch[p * pieces : (p + 1) * pieces] for p in range(4)]
    (
        rhs_v, diag_f, tile_f, diag_hi, diag_lo, tile_hi, tile_lo, solved, sol_v,
        send1, send2, recv2, own, send3, update, share, names, places_v, table, shares,
        load_sem, out_sem, s1_send, s1_recv, s2_send, s2_recv, s3_send, s3_recv,
        n_send, n_recv, n_copy, o_send, o_recv,
    ) = scratch[4 * pieces :]
    size, width = rhs.shape[1], rhs.shape[2]
    half, hubs = n // 2, n // 4
    block = size // pieces
    packed = block // 2
    rows = packed // hubs
    me = lax.axis_index("rows")
    side = me // half
    base = side * half
    pos = me - base
    first_hub = (1 - side) * hubs
    is_hub = jnp.logical_and(pos >= first_hub, pos < first_hub + hubs)
    hub = pos - first_hub
    opposite = (1 - side) * half
    peer = me + hubs * (1 - 2 * side)

    barrier = pltpu.get_barrier_semaphore()
    for j in range(1, n):
        pl.semaphore_signal(barrier, inc=1, device_id={"rows": lax.rem(me + j, n)})

    def await_bytes(ref, sem):
        pltpu.make_async_copy(ref, ref, sem).wait()

    loads = []

    def load(source, target):
        loads.append(pltpu.make_async_copy(source, target, load_sem.at[len(loads)]))

    for level in range(3):
        load(rhs.at[level], rhs_v.at[level])
        load(diag.at[level], diag_f.at[level])
        if level < 2:
            for k in range(2):
                load(tiles.at[level, k], tile_f.at[level, k])
    for copy in loads[:4]:
        copy.start()

    strip = size // 8

    def split_into(source, high_ref, low_ref):
        def step(i, carry):
            at = pl.ds(pl.multiple_of(i * strip, strip), strip)
            high, low = split(source[at, :])
            high_ref[at, :] = high
            low_ref[at, :] = low
            return carry
        lax.fori_loop(0, 8, step, 0)

    def ready_diag(level):
        loads[4 * level].wait()
        loads[4 * level + 1].wait()
        split_into(diag_f.at[level], diag_hi.at[level], diag_lo.at[level])

    def ready_tiles(level):
        for k in range(2):
            loads[4 * level + 2 + k].wait()
            split_into(tile_f.at[level, k], tile_hi.at[level, k], tile_lo.at[level, k])

    def left(shape):
        return lax.broadcasted_iota(jnp.int32, shape, 1) < width // 2

    def swap(value):
        return pltpu.roll(value, width // 2, 1)

    def twice(value, h):
        low, high = (value, swap(value)) if h == 0 else (swap(value), value)
        return jnp.where(left(value.shape), low, high)

    def keep(h, value):
        high, low = split(value)
        mask = left(value.shape)
        both = jnp.where(mask, high.astype(jnp.float32), low.astype(jnp.float32))
        solved[h, :, :width] = both.astype(jnp.bfloat16)
        solved[h, :, width:] = high

    def multiply(high, low, h):
        wide = jnp.dot(high, solved[h, :, :width], preferred_element_type=jnp.float32)
        return wide + swap(wide) + jnp.dot(low, solved[h, :, width:], preferred_element_type=jnp.float32)

    def solve(level, h, current):
        keep(h, current)
        for c in range(pieces):
            at = pl.ds(c * block, block)
            sol_v[h, at, :] = multiply(diag_hi[level, at, :], diag_lo[level, at, :], h)
        value = sol_v[h]
        keep(h, value)
        if h == 0:
            mixed = jnp.where(left(value.shape), value, rhs_v[level])
        else:
            mixed = jnp.where(left(value.shape), rhs_v[level], value)
        rhs_v[level] = mixed

    def keep_all(value):
        high, low = split(value)
        solved[0, :, :width] = high
        solved[0, :, width:] = low

    def multiply_all(high, low):
        wide = jnp.dot(high, solved[0], preferred_element_type=jnp.float32)
        other = jnp.dot(low, solved[0, :, :width], preferred_element_type=jnp.float32)
        return wide[:, :width] + wide[:, width:] + other

    def result_copy(level):
        return pltpu.make_async_copy(rhs_v.at[level], sol.at[level], out_sem.at[level])

    def names_copy(to):
        return pltpu.make_async_remote_copy(
            src_ref=share, dst_ref=names.at[pos], send_sem=n_send, recv_sem=n_recv,
            device_id={"rows": base + first_hub + to})

    def first(p, c, to):
        return pltpu.make_async_remote_copy(
            src_ref=send1.at[p, c, :, pl.ds(pl.multiple_of(to * rows, rows), rows), :],
            dst_ref=stage1[p][c].at[pl.ds(2 * pos, 2)],
            send_sem=s1_send.at[p], recv_sem=s1_recv.at[p, c],
            device_id={"rows": base + first_hub + to})

    def second(p, c):
        return pltpu.make_async_remote_copy(
            src_ref=send2.at[p, c], dst_ref=recv2.at[p, c],
            send_sem=s2_send.at[p, c], recv_sem=s2_recv.at[p, c], device_id={"rows": peer})

    def third(p, c, owner):
        at = pl.ds(pl.multiple_of(hub * rows, rows), rows)
        return pltpu.make_async_remote_copy(
            src_ref=send3.at[p, c, owner], dst_ref=update.at[p, c, at, :],
            send_sem=s3_send.at[p], recv_sem=s3_recv.at[p],
            device_id={"rows": base + owner})

    def send_piece(p, c):
        @pl.when(is_hub)
        def _():
            at = pl.ds(pl.multiple_of(hub * rows, rows), rows)
            stage1[p][c][pl.ds(2 * pos, 2)] = send1[p, c, :, at, :]

        @pl.when(jnp.logical_not(is_hub))
        def _():
            first(p, c, lax.rem(pos, hubs)).start()

        for j in range(1, hubs):
            first(p, c, lax.rem(pos + j, hubs)).start()

    def send_products(p):
        t, h = p // 2, p % 2
        for c in range(pieces):
            at = pl.ds(c * block, block)
            for k in range(2):
                value = multiply(tile_hi[t, k, at, :], tile_lo[t, k, at, :], h)
                top, bottom = value[:packed], value[packed:]
                send1[p, c, k] = jnp.where(left(top.shape), top, bottom)
            send_piece(p, c)

    def first_level():
        keep_all(rhs_v[0])
        for c in range(pieces):
            at = pl.ds(c * block, block)
            rhs_v[0, at, :] = multiply_all(diag_hi[0, at, :], diag_lo[0, at, :])
        result_copy(0).start()
        keep_all(rhs_v[0])

    def first_products():
        for c in range(pieces):
            at = pl.ds(c * block, block)
            for k in range(2):
                value = multiply_all(tile_hi[0, k, at, :], tile_lo[0, k, at, :])
                top, bottom = value[:packed], value[packed:]
                mask = left(top.shape)
                send1[0, c, k] = jnp.where(mask, top, swap(bottom))
                send1[1, c, k] = jnp.where(mask, swap(top), bottom)
            send_piece(0, c)
        for c in range(pieces):
            send_piece(1, c)

    def build_table():
        await_bytes(names.at[pl.ds(0, half - 1)], n_recv)
        shape = places_v.shape
        target = lax.broadcasted_iota(jnp.int32, shape, 0)
        turn = lax.broadcasted_iota(jnp.int32, shape, 1) % CAP
        count = jnp.zeros(shape, jnp.int32)
        place = jnp.full(shape, n, jnp.int32)
        for q in range(n):
            hit = jnp.broadcast_to(names[q // 2, q % 2 : q % 2 + 1, :], shape) == target
            place = jnp.where(jnp.logical_and(hit, count == turn), q, place)
            count = count + jnp.where(hit, 1, 0)
        places_v[...] = place
        move = pltpu.make_async_copy(places_v, table, n_copy)
        move.start()
        move.wait()

    def add_up(p, c, start, out):
        buffer, column = stage1[p][c], p // 2 * CAP

        for i in range(half):
            d = start + i
            total = buffer[table[d, column]] + buffer[table[d, column + 1]]
            out[i] = total + (buffer[table[d, column + 2]] + buffer[table[d, column + 3]])

    def finish(step):
        p, c = step // pieces, step % pieces
        second(p, c).wait_recv()

        for i in range(half):
            send3[p, c, i] = own[step % 2, i] + recv2[p, c, i]
        for j in range(1, half):
            third(p, c, lax.rem(pos + j, half)).start()
        update[p, c, pl.ds(pl.multiple_of(hub * rows, rows), rows), :] = send3[p, c, pos]

    def hub_step(step):
        p, c = step // pieces, step % pieces

        @pl.when(is_hub)
        def _():
            if step == 0:
                build_table()
            if step < 4 * pieces:
                await_bytes(stage1[p][c].at[pl.ds(0, 2 * (half - 1))], s1_recv.at[p, c])
                add_up(p, c, opposite, send2.at[p, c])
                second(p, c).start()
                add_up(p, c, base, own.at[step % 2])
            if step > 0:
                finish(step - 1)

    def receive(p):
        t, h = p // 2, p % 2
        @pl.when(is_hub)
        def _():
            await_bytes(update.at[p, :, pl.ds(0, packed - rows), :], s3_recv.at[p])

        @pl.when(jnp.logical_not(is_hub))
        def _():
            await_bytes(update.at[p], s3_recv.at[p])

        parts = []
        for c in range(pieces):
            value = update[p, c]
            parts += [twice(value, 0), twice(value, 1)]
        solve(t + 1, h, twice(rhs_v[t + 1], h) - jnp.concatenate(parts, axis=0))

    line = lax.broadcasted_iota(jnp.int32, share.shape, 0)
    lane = lax.broadcasted_iota(jnp.int32, share.shape, 1)
    value = jnp.zeros(share.shape, jnp.int32)
    for k in range(2):
        value = jnp.where(line == k, jnp.where(lane < CAP, dest[0, k], dest[1, k]), value)
    share[...] = value
    for p in range(4):
        for c in range(pieces):
            stage1[p][c][n] = jnp.zeros((rows, width), jnp.float32)

    ready_diag(0)
    first_level()
    pl.semaphore_wait(barrier, n - 1)
    @pl.when(is_hub)
    def _():
        names[pos] = share[...]

    @pl.when(jnp.logical_not(is_hub))
    def _():
        names_copy(lax.rem(pos, hubs)).start()

    for j in range(1, hubs):
        names_copy(lax.rem(pos + j, hubs)).start()
    ready_tiles(0)
    for copy in loads[4:]:
        copy.start()
    first_products()

    for step in range(4 * pieces + 1):
        hub_step(step)
        if step == 0:
            ready_diag(1)
            ready_tiles(1)
        if step == 2 * pieces:
            ready_diag(2)
        if step == pieces + 1:
            receive(0)
            send_products(2)
        if step == 2 * pieces + 1:
            receive(1)
            result_copy(1).start()
            send_products(3)
        if step == 3 * pieces + 1:
            receive(2)
    receive(3)
    result_copy(2).start()

    high, low = split(jnp.broadcast_to(weight[...].reshape(1, size), (16, size)))
    part = [multiply(high, low, h)[:8] for h in range(2)]
    shares[me] = jnp.where(left(part[0].shape), part[0], part[1])

    for j in range(1, n):
        pltpu.make_async_remote_copy(
            src_ref=shares.at[me], dst_ref=shares.at[me], send_sem=o_send,
            recv_sem=o_recv, device_id={"rows": lax.rem(me + j, n)}).start()

    @pl.when(is_hub)
    def _():
        await_bytes(names.at[pl.ds(0, hubs - 1)], n_send)
        for p in range(4):
            await_bytes(send1.at[p, :, :, pl.ds(0, packed - rows), :], s1_send.at[p])
            await_bytes(send3.at[p, :, pl.ds(0, half - 1)], s3_send.at[p])
            for c in range(pieces):
                second(p, c).wait_send()

    @pl.when(jnp.logical_not(is_hub))
    def _():
        await_bytes(names.at[pl.ds(0, hubs)], n_send)
        for p in range(4):
            await_bytes(send1.at[p], s1_send.at[p])

    await_bytes(shares.at[pl.ds(0, n - 1)], o_send)
    await_bytes(shares.at[pl.ds(0, n - 1)], o_recv)
    total = shares[0]
    for other in range(1, n):
        total = total + shares[other]
    observed[...] = total[:1]
    for level in range(3):
        result_copy(level).wait()


def hand_over_kernel(parts, source, target, sem):
    levels, size = source.shape[:2]
    step = size // parts
    copies = [
        pltpu.make_async_copy(
            source.at[level, pl.ds(i * step, step), :], target.at[level, pl.ds(i * step, step), :],
            sem.at[level * parts + i])
        for level in range(levels) for i in range(parts)
    ]
    for copy in copies:
        copy.start()
    for copy in copies:
        copy.wait()


def hand_over(value):
    parts = 4
    return pl.pallas_call(
        functools.partial(hand_over_kernel, parts),
        out_shape=jax.ShapeDtypeStruct(value.shape, value.dtype),
        in_specs=[pl.BlockSpec(memory_space=pl.ANY)],
        out_specs=pl.BlockSpec(memory_space=pl.ANY),
        scratch_shapes=[pltpu.SemaphoreType.DMA((value.shape[0] * parts,))],
        cost_estimate=pl.CostEstimate(flops=0, bytes_accessed=8 * value.size, transcendentals=0),
    )(value)


def body(rhs, diag_inv, tiles, dest, obs_weight):
    n = lax.axis_size("rows")
    size, width = rhs.shape[1], rhs.shape[2]
    half, hubs = n // 2, n // 4
    pieces = PIECES
    packed = size // pieces // 2
    rows = packed // hubs
    f32, bf16 = jnp.float32, jnp.bfloat16
    dma = pltpu.SemaphoreType.DMA
    vmem = pl.BlockSpec(memory_space=pltpu.VMEM)
    anywhere = pl.BlockSpec(memory_space=pl.ANY)
    sol, observed = pl.pallas_call(
        functools.partial(kernel, n, pieces),
        out_shape=(
            jax.ShapeDtypeStruct((3, size, width), f32),
            jax.ShapeDtypeStruct((1, width), f32),
        ),
        in_specs=[anywhere, vmem, pl.BlockSpec(memory_space=pltpu.SMEM), anywhere, anywhere],
        out_specs=(anywhere, vmem),
        scratch_shapes=[pltpu.VMEM((n + 1, rows, width), f32) for _ in range(4 * pieces)] + [
            pltpu.VMEM((3, size, width), f32),
            pltpu.VMEM((3, size, size), f32),
            pltpu.VMEM((2, 2, size, size), f32),
            pltpu.VMEM((3, size, size), bf16),
            pltpu.VMEM((3, size, size), bf16),
            pltpu.VMEM((2, 2, size, size), bf16),
            pltpu.VMEM((2, 2, size, size), bf16),
            pltpu.VMEM((2, size, 2 * width), bf16),
            pltpu.VMEM((2, size, width), f32),
            pltpu.VMEM((4, pieces, 2, packed, width), f32),
            pltpu.VMEM((4, pieces, half, rows, width), f32),
            pltpu.VMEM((4, pieces, half, rows, width), f32),
            pltpu.VMEM((2, half, rows, width), f32),
            pltpu.VMEM((4, pieces, half, rows, width), f32),
            pltpu.VMEM((4, pieces, packed, width), f32),
            pltpu.VMEM((8, 128), jnp.int32),
            pltpu.VMEM((half, 8, 128), jnp.int32),
            pltpu.VMEM((n, 128), jnp.int32),
            pltpu.SMEM((n, 128), jnp.int32),
            pltpu.VMEM((n, 8, width), f32),
            dma((10,)), dma((3,)),
            dma((4,)), dma((4, pieces)),
            dma((4, pieces)), dma((4, pieces)),
            dma((4,)), dma((4,)),
            dma, dma, dma, dma, dma,
        ],
        compiler_params=pltpu.CompilerParams(
            collective_id=0, has_side_effects=True, vmem_limit_bytes=60 * 1024 * 1024
        ),
        cost_estimate=pl.CostEstimate(
            flops=7 * 3 * 2 * size * size * width, bytes_accessed=7 * 4 * size * size, transcendentals=0
        ),
    )(rhs, obs_weight, dest.reshape(2, 2), diag_inv, tiles)
    return hand_over(sol), observed.reshape(width)


def solution(mesh):
    in_specs = (
        P(None, "rows", "parts"),
        P(None, "rows", None),
        P(None, "rows", None, None),
        P(None, "rows", None),
        P("rows"),
    )
    out_specs = (P(None, "rows", "parts"), P("parts"))
    return jax.shard_map(body, mesh=mesh, in_specs=in_specs, out_specs=out_specs, check_vma=False)
```
